512 devices in a mesh: freq: 16 (over x_hi, y), tx: 4 (over x_lo, core), ty: 8 (over z).
Axes of the slice: x: 4 (x_hi: 2, x_lo: 2; x = x_hi * 2 + x_lo), y: 8, z: 8, core: 2. Of those that a mesh axis runs over, the one named last changes fastest.
Arguments:
- wavefield: float32 [2, 32, 128, 2048], P(None, 'freq', 'tx', 'ty'), may hold values from -6 to 6
- coef_table: float32 [2, 32, 9, 32], P(None, 'freq'), may hold values from -2.4 to 2.4
- velocity_bins: int32 [4, 128, 2048], P(None, 'tx', 'ty'), may hold values from 0 to 30
- slab_fracs: float32 [32, 128, 2048], P('freq', 'tx', 'ty'), may hold values from 0 to 1
- owners: int32 [4], replicated, may hold values from 0 to 31
Outputs:
- wave_out: float32 [2, 32, 128, 2048], P(None, 'freq', 'tx', 'ty')
- images: float32 [4, 128, 2048], P(None, 'tx', 'ty')
The draws below stay inside these ranges and needn't reach their ends.
All inputs are finite; a program needn't handle non-finite values.
Results may differ from the reference program's by a relative error of at most 0.0003.
Values sent between devices are 32-bit elements; how exact they have to be, the bound alone decides.
A program may use at most 64 MiB of HBM per device.

```python
import math
import jax
import jax.numpy as jnp
from jax import lax

DEGREE = 8
NBINS = 32
STEPS = 4
FREQS = 32
NX = 128
NY = 2048
SLABS = 32


def plant(entries, key, least, high):
    place = [jax.random.randint(jax.random.fold_in(key, axis), (), 0, length) for axis, length in enumerate(entries.shape)]
    main_axis = entries.shape.index(max(entries.shape))
    beside = place[:main_axis] + [(place[main_axis] + 1) % entries.shape[main_axis]] + place[main_axis + 1:]
    return entries.at[tuple(place)].set(least).at[tuple(beside)].set(high)


def steps_of(key, extent, cuts, low, largest):
    gain, own = 1.0, jax.random.fold_in(key, 6)
    for axis_at, shards_of in cuts:
        heights = jnp.exp(jax.random.uniform(jax.random.fold_in(own, axis_at), (shards_of,), jnp.float32, low / len(cuts), largest / len(cuts)))
        gain = gain * jnp.repeat(heights, extent[axis_at] // shards_of).reshape([-1 if axis == axis_at else 1 for axis in range(len(extent))])
    return gain


def gaussian(rng, shape, deviation, most, cuts=(), kind=jnp.bfloat16):
    drawn = jax.random.normal(rng, shape, jnp.float32) * deviation
    if len(cuts) > 0:
        drawn = steps_of(rng, shape, cuts, -0.22, 0.18) * drawn
    return jnp.clip(drawn, min=-most, max=most).astype(kind)


def setup_inputs(seed: int = 0) -> dict:
    keys = jax.random.split(jax.random.key(seed), 6)
    return {
        "wavefield": gaussian(keys[0], (2, FREQS, NX, NY), 1.0, 6.0, ((1, 16), (2, 4), (3, 8)), jnp.float32),
        "coef_table": gaussian(keys[1], (2, FREQS, DEGREE + 1, NBINS), 0.4, 2.4, ((1, 16),), jnp.float32),
        "velocity_bins": plant(jax.random.randint(keys[2], (STEPS, NX, NY), 0, NBINS - 1), jax.random.fold_in(keys[2], 1), 0, (NBINS - 1) - 1).astype(jnp.int32),
        "slab_fracs": jnp.clip(1.0 * jax.random.uniform(keys[3], (SLABS, NX, NY), jnp.float32) ** steps_of(keys[3], (SLABS, NX, NY), ((0, 16), (1, 4), (2, 8)), -0.2, 0.2), 0.0, 1.0),
        "owners": plant(jax.random.randint(keys[4], (STEPS,), 0, SLABS), jax.random.fold_in(keys[4], 1), 0, SLABS - 1).astype(jnp.int32),
    }


def smooth(padded):
    along_x = 0.25 * padded[:, :, :-2, :] + 0.5 * padded[:, :, 1:-1, :] + 0.25 * padded[:, :, 2:, :]
    along_y = 0.25 * along_x[:, :, :, :-2] + 0.5 * along_x[:, :, :, 1:-1] + 0.25 * along_x[:, :, :, 2:]
    return 2.0 * along_y - padded[:, :, 1:-1, 1:-1]

def mcclellan(values):
    return smooth(jnp.pad(values, ((0, 0), (0, 0), (1, 1), (1, 1))))

def reference(wavefield, coef_table, velocity_bins, slab_fracs, owners):
    wave_now = wavefield
    levels = jnp.arange(NBINS, dtype=jnp.int32)[:, None]
    image_list = []
    for slice_index in range(STEPS):
        fraction = lax.dynamic_index_in_dim(slab_fracs, owners[slice_index], 0, keepdims=False).reshape(-1)
        bin_index = velocity_bins[slice_index].reshape(-1).astype(jnp.int32)
        blending = jnp.where(levels == bin_index[None, :], 1.0 - fraction[None, :], jnp.float32(0.0))
        blending = blending + jnp.where(levels == bin_index[None, :] + 1, fraction[None, :], jnp.float32(0.0))

        def weighted(power, chebyshev):
            table_rows = coef_table[:, :, power, :].reshape(2 * FREQS, NBINS)
            coeff = jnp.dot(table_rows, blending, precision=lax.Precision.HIGHEST).reshape(2, FREQS, NX, NY)
            real_part = coeff[0] * chebyshev[0] - coeff[1] * chebyshev[1]
            imag_part = coeff[0] * chebyshev[1] + coeff[1] * chebyshev[0]
            return jnp.stack([real_part, imag_part])
        previous = wave_now
        current = mcclellan(wave_now)
        summed = weighted(0, previous) + weighted(1, current)
        for power in range(2, DEGREE + 1):
            following = 2.0 * mcclellan(current) - previous
            summed = summed + weighted(power, following)
            previous, current = (current, following)
        wave_now = summed
        image_list.append(lax.optimization_barrier(jnp.sum(wave_now[0], axis=0)) / math.sqrt(FREQS))
    return (wave_now, jnp.stack(image_list))
```

```python
import functools
import math

import jax
import jax.numpy as jnp
from jax import lax
from jax.experimental import pallas as pl
from jax.experimental.pallas import tpu as pltpu
from jax.sharding import PartitionSpec as P

MESH = pl.DeviceIdType.MESH
HALO = 8
LANES = 128
GROUP = 32


def kernel(
    sizes,
    owners,
    wave,
    table,
    bins,
    slabs,
    wave_out,
    images,
    wv,
    lnd,
    pk_l,
    pk_r,
    in_r,
    in_l,
    ext3,
    mask,
    tk,
    tab_a,
    tab_d,
    co_a,
    co_d,
    src1,
    src3,
    land1,
    land3,
    dst1,
    dst3,
    halo_send,
    halo_recv,
    rs_send,
    rs_recv,
    ag_send,
    ag_recv,
):
    n, n_tx, n_ty = sizes
    me, tx, ty = lax.axis_index("freq"), lax.axis_index("tx"), lax.axis_index("ty")
    _, freqs, rows, cols = wave.shape
    steps = bins.shape[0]
    orders = table.shape[2]
    row_tiles, col_tiles = rows // 8, cols // LANES
    tiles = row_tiles * col_tiles
    chunks = src1.shape[2]
    per = tiles // chunks
    fields = 2 * freqs
    mine, group = lax.rem(me, chunks), lax.div(me, chunks) * chunks

    up, down = lax.rem(tx + n_tx - 1, n_tx), lax.rem(tx + 1, n_tx)
    left, right = lax.rem(ty + n_ty - 1, n_ty), lax.rem(ty + 1, n_ty)

    def there(x, y):
        return {"tx": x, "ty": y}

    def peer(d):
        return lax.rem(me + d, n)

    barrier = pltpu.get_barrier_semaphore()
    for d in range(1, n):
        pl.semaphore_signal(barrier, inc=1, device_id={"freq": peer(d)}, device_id_type=MESH)
    for x in (up, tx, down):
        for y in (left, ty, right):
            if x is not tx or y is not ty:
                pl.semaphore_signal(barrier, inc=1, device_id=there(x, y), device_id_type=MESH)

    def parts(g):
        return (src1.at[g // 3], land1.at[g // 3], dst1.at[g // 3]) if g in (0, 3) else (src3.at[g - 1], land3.at[g - 1], dst3.at[g - 1])

    def scatter_copy(g, d):
        src, land, _ = parts(g)
        to = peer(d)
        return pltpu.make_async_remote_copy(
            src_ref=src.at[:, lax.rem(to, chunks)],
            dst_ref=land.at[d],
            send_sem=rs_send.at[g, d],
            recv_sem=rs_recv.at[g, d],
            device_id={"freq": to},
            device_id_type=MESH,
        )

    def gather_copy(g, d):
        _, _, dst = parts(g)
        return pltpu.make_async_remote_copy(
            src_ref=dst.at[:, mine],
            dst_ref=dst.at[:, mine],
            send_sem=ag_send.at[g, d],
            recv_sem=ag_recv.at[g, d],
            device_id={"freq": group + lax.rem(mine + d, chunks)},
            device_id_type=MESH,
        )

    def gather_wait(g, d):
        _, _, dst = parts(g)
        origin = lax.rem(mine + chunks - d, chunks)
        return pltpu.make_async_remote_copy(
            src_ref=dst.at[:, origin],
            dst_ref=dst.at[:, origin],
            send_sem=ag_send.at[g, d],
            recv_sem=ag_recv.at[g, d],
            device_id={"freq": group + origin},
            device_id_type=MESH,
        )

    def scatter(g):
        for d in range(1, n):
            scatter_copy(g, d).start()

    def reduce_and_gather(g):
        src, land, dst = parts(g)
        for d in range(1, n):
            scatter_copy(g, d).wait_recv()
        total = src[:, mine]
        for d in range(1, n):
            total = total + land[d]
        dst[:, mine] = total
        for d in range(1, chunks):
            gather_copy(g, d).start()

    def gathered(g):
        for d in range(1, chunks):
            gather_wait(g, d).wait_recv()

    def tile_at(r, c):
        t = r * col_tiles + c
        return t // per, pl.ds((t % per) * 8, 8)

    def halo_copies(s):
        pieces = [
            (wv.at[s, :, :, 0:HALO], lnd.at[s, :, :, 0:HALO], there(up, ty)),
            (wv.at[s, :, :, rows - HALO : rows], lnd.at[s, :, :, HALO : 2 * HALO], there(down, ty)),
            (pk_l.at[s], in_r.at[s, 0:rows], there(tx, left)),
            (pk_r.at[s], in_l.at[s, 0:rows], there(tx, right)),
            (pk_l.at[s, 0:HALO], in_r.at[s, rows : rows + HALO], there(up, left)),
            (pk_l.at[s, rows - HALO : rows], in_r.at[s, rows + HALO : rows + 2 * HALO], there(down, left)),
            (pk_r.at[s, 0:HALO], in_l.at[s, rows : rows + HALO], there(up, right)),
            (pk_r.at[s, rows - HALO : rows], in_l.at[s, rows + HALO : rows + 2 * HALO], there(down, right)),
        ]
        return [
            pltpu.make_async_remote_copy(
                src_ref=src,
                dst_ref=dst,
                send_sem=halo_send.at[s, i],
                recv_sem=halo_recv.at[s, i],
                device_id=to,
                device_id_type=MESH,
            )
            for i, (src, dst, to) in enumerate(pieces)
        ]

    lane = lax.broadcasted_iota(jnp.int32, (rows, LANES), 1)

    def pack(s):
        packed_l = packed_r = None
        for c in range(2):
            for f in range(freqs):
                at = (c * freqs + f) * GROUP
                first = wv[s, c, f, :, 0:LANES]
                last = wv[s, c, f, :, cols - LANES : cols]
                if at == 0:
                    packed_l, packed_r = first, last
                else:
                    packed_l = jnp.where(lane // GROUP == at // GROUP, pltpu.roll(first, at, 1), packed_l)
                    packed_r = jnp.where(lane // GROUP == at // GROUP - 1, pltpu.roll(last, at, 1), packed_r)
        pk_l[s] = packed_l
        pk_r[s] = packed_r

    def send_halos(s):
        pack(s)
        for copy in halo_copies(s):
            copy.start()

    for c in range(2):
        for f in range(freqs):
            wv[0, c, f] = wave[c, f]
    pack(0)
    per_slab = slabs.shape[0]
    for j in range(steps):
        owner = owners[j]
        src = src1.at[0, 0] if j == 0 else src3.at[0, j - 1]
        for r in range(row_tiles):
            for c in range(col_tiles):
                value = jnp.zeros((8, LANES), jnp.float32)
                for i in range(per_slab):
                    tile = slabs[i, 8 * r : 8 * r + 8, LANES * c : LANES * c + LANES]
                    value = jnp.where(jnp.full((8, LANES), owner) == me * per_slab + i, tile, value)
                chunk, at = tile_at(r, c)
                src[chunk, at] = value

    pl.semaphore_wait(barrier, n - 1 + 8)
    scatter(0)
    for copy in halo_copies(0):
        copy.start()
    scatter(1)

    tab_a[...] = jnp.zeros_like(tab_a)
    for c in range(2):
        for f in range(freqs):
            tab_a[c * freqs + f, 0:orders, 0 : table.shape[3]] = table[c, f]
    for i in range(fields):
        tab_d[i] = pltpu.roll(tab_a[i], LANES - 1, 1) - tab_a[i]

    ext_rows, ext_cols = rows + 2 * HALO, cols + LANES
    r = lax.broadcasted_iota(jnp.int32, (ext_rows, ext_cols), 0)
    c = lax.broadcasted_iota(jnp.int32, (ext_rows, ext_cols), 1)
    no_down = jnp.where(tx == n_tx - 1, 1, 0)
    no_up = jnp.where(tx == 0, 1, 0)
    no_right = jnp.where(ty == n_ty - 1, 1, 0)
    no_left = jnp.where(ty == 0, 1, 0)
    outside = jnp.where(r >= rows + HALO, no_up, jnp.where(r >= rows, no_down, 0))
    outside = outside + jnp.where(c >= cols + LANES // 2, no_left, jnp.where(c >= cols, no_right, 0))
    mask[...] = jnp.where(outside > 0, 0.0, 0.25)

    def lookup(s):
        def one(i, carry):
            for r in range(row_tiles):
                for c in range(col_tiles):
                    rs, cs = slice(8 * r, 8 * r + 8), slice(LANES * c, LANES * c + LANES)
                    index = bins[s, rs, cs]
                    for k in range(orders):
                        for tab, co in ((tab_a, co_a), (tab_d, co_d)):
                            row = jnp.broadcast_to(tab[i, k : k + 1, :], (8, LANES))
                            co[i, k, rs, cs] = jnp.take_along_axis(row, index, axis=1, mode="promise_in_bounds")
            return carry

        lax.fori_loop(0, fields, one, 0)

    def smooth(v):
        v = v + pltpu.roll(v, 1, 0)
        v = v + pltpu.roll(v, ext_rows - 1, 0)
        v = v + pltpu.roll(v, 1, 1)
        return v + pltpu.roll(v, ext_cols - 1, 1)

    ext_lane = lax.broadcasted_iota(jnp.int32, (ext_rows, LANES), 1)

    def recurrence(s):
        both = jnp.where(lax.rem(ext_lane, GROUP) < GROUP // 2, in_r[s], in_l[s])
        for i in range(fields):
            ext3[i] = both if i == 0 else pltpu.roll(both, LANES - i * GROUP, 1)

        def one(i, carry):
            c, f = i // freqs, lax.rem(i, freqs)
            quarter = mask[...]
            own = jnp.concatenate([wv[s, c, f], lnd[s, c, f]], axis=0)
            t = jnp.concatenate([own, ext3[i]], axis=1) * (4.0 * quarter)
            p = None
            for k in range(1, orders):
                w = smooth(t) * quarter
                p = 0.5 * w if k == 1 else w - p
                t = p - t
                tk[k - 1, i] = t[0:rows, 0:cols]
            return carry

        lax.fori_loop(0, fields, one, 0)

    scale = 1.0 / math.sqrt(freqs * n)

    def combine(s):
        frac = dst1.at[0, 0] if s == 0 else dst3.at[0, s - 1]
        image = src1.at[1, 0] if s == steps - 1 else src3.at[1, s]
        for r in range(row_tiles):
            for c in range(col_tiles):
                rs, cs = slice(8 * r, 8 * r + 8), slice(LANES * c, LANES * c + LANES)
                chunk, at = tile_at(r, c)
                fraction = frac[chunk, at]
                summed = None
                for f in range(freqs):
                    re = im = None
                    for k in range(orders):
                        t_re = wv[s, 0, f, rs, cs] if k == 0 else tk[k - 1, f, rs, cs]
                        t_im = wv[s, 1, f, rs, cs] if k == 0 else tk[k - 1, freqs + f, rs, cs]
                        c_re = co_a[f, k, rs, cs] + fraction * co_d[f, k, rs, cs]
                        c_im = co_a[freqs + f, k, rs, cs] + fraction * co_d[freqs + f, k, rs, cs]
                        add_re = c_re * t_re - c_im * t_im
                        add_im = c_re * t_im + c_im * t_re
                        re = add_re if k == 0 else re + add_re
                        im = add_im if k == 0 else im + add_im
                    if s == steps - 1:
                        wave_out[0, f, rs, cs] = re
                        wave_out[1, f, rs, cs] = im
                    else:
                        wv[s + 1, 0, f, rs, cs] = re
                        wv[s + 1, 1, f, rs, cs] = im
                    summed = re if f == 0 else summed + re
                image[chunk, at] = summed * scale

    lookup(0)
    reduce_and_gather(0)
    for s in range(steps):
        for copy in halo_copies(s):
            copy.wait_recv()
        recurrence(s)
        if s == 0:
            gathered(0)
        if s == 1:
            gathered(1)
        combine(s)
        if s < steps - 1:
            send_halos(s + 1)
            if s == 0:
                reduce_and_gather(1)
            if s == steps - 2:
                scatter(2)
            lookup(s + 1)

    scatter(3)
    reduce_and_gather(2)
    reduce_and_gather(3)

    def put_image(j, src):
        for r in range(row_tiles):
            for c in range(col_tiles):
                chunk, at = tile_at(r, c)
                images[j, 8 * r : 8 * r + 8, LANES * c : LANES * c + LANES] = src[chunk, at]

    gathered(2)
    for j in range(steps - 1):
        put_image(j, dst3.at[1, j])
    for s in range(steps):
        for copy in halo_copies(s):
            copy.wait_send()
    for g in range(4):
        for d in range(1, n):
            scatter_copy(g, d).wait_send()
        for d in range(1, chunks):
            if g < 3:
                gather_copy(g, d).wait_send()
    gathered(3)
    put_image(steps - 1, dst1.at[1, 0])
    for d in range(1, chunks):
        gather_copy(3, d).wait_send()


def solution(mesh):
    n, n_tx, n_ty = (mesh.shape[axis] for axis in ("freq", "tx", "ty"))

    def on_device(wavefield, coef_table, velocity_bins, slab_fracs, owners):
        _, freqs, rows, cols = wavefield.shape
        orders = coef_table.shape[2]
        steps = velocity_bins.shape[0]
        tiles = rows // 8 * (cols // LANES)
        chunks = min(n, tiles)
        chunk = (chunks, tiles // chunks * 8, LANES)
        fields = 2 * freqs
        ext_rows, ext_cols = rows + 2 * HALO, cols + LANES
        f32 = jnp.float32
        vmem = pl.BlockSpec(memory_space=pltpu.VMEM)
        dma = pltpu.SemaphoreType.DMA
        return pl.pallas_call(
            functools.partial(kernel, (n, n_tx, n_ty)),
            out_shape=(
                jax.ShapeDtypeStruct(wavefield.shape, f32),
                jax.ShapeDtypeStruct((steps, rows, cols), f32),
            ),
            in_specs=[pl.BlockSpec(memory_space=pltpu.SMEM)] + [vmem] * 4,
            out_specs=(vmem, vmem),
            scratch_shapes=[
                pltpu.VMEM((steps, 2, freqs, rows, cols), f32),
                pltpu.VMEM((steps, 2, freqs, 2 * HALO, cols), f32),
                pltpu.VMEM((steps, rows, LANES), f32),
                pltpu.VMEM((steps, rows, LANES), f32),
                pltpu.VMEM((steps, ext_rows, LANES), f32),
                pltpu.VMEM((steps, ext_rows, LANES), f32),
                pltpu.VMEM((fields, ext_rows, LANES), f32),
                pltpu.VMEM((ext_rows, ext_cols), f32),
                pltpu.VMEM((orders - 1, fields, rows, cols), f32),
                pltpu.VMEM((fields, 16, LANES), f32),
                pltpu.VMEM((fields, 16, LANES), f32),
                pltpu.VMEM((fields, orders, rows, cols), f32),
                pltpu.VMEM((fields, orders, rows, cols), f32),
                pltpu.VMEM((2, 1) + chunk, f32),
                pltpu.VMEM((2, steps - 1) + chunk, f32),
                pltpu.VMEM((2, n, 1) + chunk[1:], f32),
                pltpu.VMEM((2, n, steps - 1) + chunk[1:], f32),
                pltpu.VMEM((2, 1) + chunk, f32),
                pltpu.VMEM((2, steps - 1) + chunk, f32),
                dma((steps, 8)),
                dma((steps, 8)),
                dma((4, n)),
                dma((4, n)),
                dma((4, chunks)),
                dma((4, chunks)),
            ],
            compiler_params=pltpu.CompilerParams(
                collective_id=0, has_side_effects=True, vmem_limit_bytes=32 * 1024 * 1024
            ),
        )(owners, wavefield, coef_table, velocity_bins, slab_fracs)

    in_specs = (
        P(None, "freq", "tx", "ty"),
        P(None, "freq", None, None),
        P(None, "tx", "ty"),
        P("freq", "tx", "ty"),
        P(),
    )
    out_specs = (P(None, "freq", "tx", "ty"), P(None, "tx", "ty"))
    return jax.shard_map(on_device, mesh=mesh, in_specs=in_specs, out_specs=out_specs, check_vma=False)
```

```python
import functools
import math

import jax
import jax.numpy as jnp
from jax import lax
from jax.experimental import pallas as pl
from jax.experimental.pallas import tpu as pltpu
from jax.sharding import PartitionSpec as P

MESH = pl.DeviceIdType.MESH
HALO = 8
LANES = 128
GROUP = 32


def kernel(
    sizes,
    owners,
    wave_hbm,
    table,
    bins_hbm,
    slabs_hbm,
    wave_out,
    images,
    bins,
    slabs,
    wv,
    lnd,
    pk_l,
    pk_r,
    in_r,
    in_l,
    ext3,
    mask,
    tk,
    tab_a,
    tab_d,
    co_a,
    co_d,
    src1,
    src3,
    land1,
    land3,
    dst1,
    dst3,
    in_sem,
    halo_send,
    halo_recv,
    rs_send,
    rs_recv,
    ag_send,
    ag_recv,
):
    n, n_tx, n_ty = sizes
    me, tx, ty = lax.axis_index("freq"), lax.axis_index("tx"), lax.axis_index("ty")
    _, freqs, rows, cols = wave_hbm.shape
    steps = bins.shape[0]
    orders = table.shape[1]
    row_tiles, col_tiles = rows // 8, cols // LANES
    tiles = row_tiles * col_tiles
    chunks = src1.shape[2]
    per = tiles // chunks
    fields = 2 * freqs
    mine, group = lax.rem(me, chunks), lax.div(me, chunks) * chunks

    up, down = lax.rem(tx + n_tx - 1, n_tx), lax.rem(tx + 1, n_tx)
    left, right = lax.rem(ty + n_ty - 1, n_ty), lax.rem(ty + 1, n_ty)

    def there(x, y):
        return {"tx": x, "ty": y}

    def peer(d):
        return lax.rem(me + d, n)

    inputs = [
        pltpu.make_async_copy(slabs_hbm, slabs, in_sem.at[0]),
        pltpu.make_async_copy(wave_hbm, wv.at[0], in_sem.at[1]),
        pltpu.make_async_copy(bins_hbm, bins, in_sem.at[2]),
    ]
    for copy in inputs:
        copy.start()

    barrier = pltpu.get_barrier_semaphore()
    for d in range(1, n):
        pl.semaphore_signal(barrier, inc=1, device_id={"freq": peer(d)}, device_id_type=MESH)
    for x in (up, tx, down):
        for y in (left, ty, right):
            if x is not tx or y is not ty:
                pl.semaphore_signal(barrier, inc=1, device_id=there(x, y), device_id_type=MESH)

    def parts(g):
        return (src1.at[g // 3], land1.at[g // 3], dst1.at[g // 3]) if g in (0, 3) else (src3.at[g - 1], land3.at[g - 1], dst3.at[g - 1])

    def scatter_copy(g, d):
        src, land, _ = parts(g)
        to = peer(d)
        return pltpu.make_async_remote_copy(
            src_ref=src.at[:, lax.rem(to, chunks)],
            dst_ref=land.at[d],
            send_sem=rs_send.at[g],
            recv_sem=rs_recv.at[g],
            device_id={"freq": to},
            device_id_type=MESH,
        )

    def gather_copy(g, d):
        _, _, dst = parts(g)
        return pltpu.make_async_remote_copy(
            src_ref=dst.at[:, mine],
            dst_ref=dst.at[:, mine],
            send_sem=ag_send.at[g],
            recv_sem=ag_recv.at[g],
            device_id={"freq": group + lax.rem(mine + d, chunks)},
            device_id_type=MESH,
        )

    def wait_for(ref, sem):
        pltpu.make_async_copy(ref, ref, sem).wait()

    def scatter(g):
        for d in range(1, n):
            scatter_copy(g, d).start()

    def reduce_and_gather(g):
        src, land, dst = parts(g)
        wait_for(land.at[1:n], rs_recv.at[g])
        total = src[:, mine]
        for d in range(1, n):
            total = total + land[d]
        dst[:, mine] = total
        for d in range(1, chunks):
            gather_copy(g, d).start()

    def gathered(g):
        wait_for(parts(g)[2].at[:, 1:chunks], ag_recv.at[g])

    def tile_at(r, c):
        t = r * col_tiles + c
        return t // per, pl.ds((t % per) * 8, 8)

    def halo_copies(s):
        pieces = [
            (0, wv.at[s, :, :, 0:HALO], lnd.at[s, :, :, 0:HALO], there(up, ty)),
            (0, wv.at[s, :, :, rows - HALO : rows], lnd.at[s, :, :, HALO : 2 * HALO], there(down, ty)),
            (1, pk_l.at[s], in_r.at[s, 0:rows], there(tx, left)),
            (2, pk_r.at[s], in_l.at[s, 0:rows], there(tx, right)),
            (1, pk_l.at[s, 0:HALO], in_r.at[s, rows : rows + HALO], there(up, left)),
            (1, pk_l.at[s, rows - HALO : rows], in_r.at[s, rows + HALO : rows + 2 * HALO], there(down, left)),
            (2, pk_r.at[s, 0:HALO], in_l.at[s, rows : rows + HALO], there(up, right)),
            (2, pk_r.at[s, rows - HALO : rows], in_l.at[s, rows + HALO : rows + 2 * HALO], there(down, right)),
        ]
        return [
            pltpu.make_async_remote_copy(
                src_ref=src,
                dst_ref=dst,
                send_sem=halo_send.at[s, i],
                recv_sem=halo_recv.at[s, i],
                device_id=to,
                device_id_type=MESH,
            )
            for i, src, dst, to in pieces
        ]

    def halo_wait(s, sems):
        for i, landing in enumerate((lnd, in_r, in_l)):
            wait_for(landing.at[s], sems.at[s, i])

    lane = lax.broadcasted_iota(jnp.int32, (rows, LANES), 1)

    def pack(s):
        packed_l = packed_r = None
        for c in range(2):
            for f in range(freqs):
                at = (c * freqs + f) * GROUP
                first = wv[s, c, f, :, 0:LANES]
                last = wv[s, c, f, :, cols - LANES : cols]
                if at == 0:
                    packed_l, packed_r = first, last
                else:
                    packed_l = jnp.where(lane // GROUP == at // GROUP, pltpu.roll(first, at, 1), packed_l)
                    packed_r = jnp.where(lane // GROUP == at // GROUP - 1, pltpu.roll(last, at, 1), packed_r)
        pk_l[s] = packed_l
        pk_r[s] = packed_r

    def send_halos(s):
        pack(s)
        for copy in halo_copies(s):
            copy.start()

    inputs[0].wait()
    per_slab = slabs.shape[0]
    for j in range(steps):
        owner = owners[j]
        src = src1.at[0, 0] if j == 0 else src3.at[0, j - 1]
        for r in range(row_tiles):
            for c in range(col_tiles):
                value = jnp.zeros((8, LANES), jnp.float32)
                for i in range(per_slab):
                    tile = slabs[i, 8 * r : 8 * r + 8, LANES * c : LANES * c + LANES]
                    value = jnp.where(jnp.full((8, LANES), owner) == me * per_slab + i, tile, value)
                chunk, at = tile_at(r, c)
                src[chunk, at] = value

    inputs[1].wait()
    pack(0)
    pl.semaphore_wait(barrier, n - 1 + 8)
    scatter(0)
    for copy in halo_copies(0):
        copy.start()
    scatter(1)

    tab_a[...] = jnp.zeros_like(tab_a)
    for c in range(2):
        for f in range(freqs):
            tab_a[c * freqs + f, 0:orders, 0 : table.shape[3]] = table[c, :, f]
    for i in range(fields):
        tab_d[i] = pltpu.roll(tab_a[i], LANES - 1, 1) - tab_a[i]

    ext_rows, ext_cols = rows + 2 * HALO, cols + LANES
    r = lax.broadcasted_iota(jnp.int32, (ext_rows, ext_cols), 0)
    c = lax.broadcasted_iota(jnp.int32, (ext_rows, ext_cols), 1)
    no_down = jnp.where(tx == n_tx - 1, 1, 0)
    no_up = jnp.where(tx == 0, 1, 0)
    no_right = jnp.where(ty == n_ty - 1, 1, 0)
    no_left = jnp.where(ty == 0, 1, 0)
    outside = jnp.where(r >= rows + HALO, no_up, jnp.where(r >= rows, no_down, 0))
    outside = outside + jnp.where(c >= cols + LANES // 2, no_left, jnp.where(c >= cols, no_right, 0))
    mask[...] = jnp.where(outside > 0, 0.0, 0.25)

    def lookup(s):
        def one(i, carry):
            for r in range(row_tiles):
                for c in range(col_tiles):
                    rs, cs = slice(8 * r, 8 * r + 8), slice(LANES * c, LANES * c + LANES)
                    index = bins[s, rs, cs]
                    for k in range(orders):
                        for tab, co in ((tab_a, co_a), (tab_d, co_d)):
                            row = jnp.broadcast_to(tab[i, k : k + 1, :], (8, LANES))
                            co[i, k, rs, cs] = jnp.take_along_axis(row, index, axis=1, mode="promise_in_bounds")
            return carry

        lax.fori_loop(0, fields, one, 0)

    ext_lane = lax.broadcasted_iota(jnp.int32, (ext_rows, LANES), 1)

    def recurrence(s):
        both = jnp.where(lax.rem(ext_lane, GROUP) < GROUP // 2, in_r[s], in_l[s])
        for i in range(fields):
            ext3[i] = both if i == 0 else pltpu.roll(both, LANES - i * GROUP, 1)

        for i in range(fields):
            c, f = i // freqs, i % freqs
            own = jnp.concatenate([wv[s, c, f], lnd[s, c, f]], axis=0)
            tk[0, i] = jnp.concatenate([own, ext3[i]], axis=1) * (4.0 * mask[...])
        for k in range(1, orders):
            twice, summed, moved = [], [], []
            for i in range(fields):
                t = tk[k - 1, i]
                twice.append(t + t)
                summed.append(twice[i] + (pltpu.roll(t, 1, 0) + pltpu.roll(t, ext_rows - 1, 0)))
            for i in range(fields):
                moved.append(pltpu.roll(summed[i], 1, 1) + pltpu.roll(summed[i], ext_cols - 1, 1))
            for i in range(fields):
                w = (summed[i] + summed[i] + moved[i]) * mask[...]
                if k == 1:
                    tk[k, i] = 0.5 * (w - twice[i])
                else:
                    tk[k, i] = (w - tk[k - 2, i]) - twice[i]

    scale = 1.0 / math.sqrt(freqs * n)

    def combine(s):
        frac = dst1.at[0, 0] if s == 0 else dst3.at[0, s - 1]
        image = src1.at[1, 0] if s == steps - 1 else src3.at[1, s]
        for r in range(row_tiles):
            for c in range(col_tiles):
                rs, cs = slice(8 * r, 8 * r + 8), slice(LANES * c, LANES * c + LANES)
                chunk, at = tile_at(r, c)
                fraction = frac[chunk, at]
                summed = None
                for f in range(freqs):
                    re = im = None
                    for k in range(orders):
                        t_re = tk[k, f, rs, cs]
                        t_im = tk[k, freqs + f, rs, cs]
                        c_re = co_a[f, k, rs, cs] + fraction * co_d[f, k, rs, cs]
                        c_im = co_a[freqs + f, k, rs, cs] + fraction * co_d[freqs + f, k, rs, cs]
                        add_re = c_re * t_re - c_im * t_im
                        add_im = c_re * t_im + c_im * t_re
                        re = add_re if k == 0 else re + add_re
                        im = add_im if k == 0 else im + add_im
                    if s == steps - 1:
                        wave_out[0, f, rs, cs] = re
                        wave_out[1, f, rs, cs] = im
                    else:
                        wv[s + 1, 0, f, rs, cs] = re
                        wv[s + 1, 1, f, rs, cs] = im
                    summed = re if f == 0 else summed + re
                image[chunk, at] = summed * scale

    inputs[2].wait()
    lookup(0)
    reduce_and_gather(0)
    for s in range(steps):
        halo_wait(s, halo_recv)
        recurrence(s)
        if s == 0:
            gathered(0)
        if s == 1:
            gathered(1)
        combine(s)
        if s < steps - 1:
            send_halos(s + 1)
            if s == 0:
                reduce_and_gather(1)
            if s == steps - 2:
                scatter(2)
            lookup(s + 1)

    scatter(3)
    reduce_and_gather(2)
    reduce_and_gather(3)

    def put_image(j, src):
        for r in range(row_tiles):
            for c in range(col_tiles):
                chunk, at = tile_at(r, c)
                images[j, 8 * r : 8 * r + 8, LANES * c : LANES * c + LANES] = src[chunk, at]

    gathered(2)
    for j in range(steps - 1):
        put_image(j, dst3.at[1, j])
    for s in range(steps):
        halo_wait(s, halo_send)
    for g in range(4):
        wait_for(parts(g)[1].at[1:n], rs_send.at[g])
        if g < 3:
            wait_for(parts(g)[2].at[:, 1:chunks], ag_send.at[g])
    gathered(3)
    put_image(steps - 1, dst1.at[1, 0])
    wait_for(dst1.at[1, :, 1:chunks], ag_send.at[3])


def solution(mesh):
    n, n_tx, n_ty = (mesh.shape[axis] for axis in ("freq", "tx", "ty"))

    def on_device(wavefield, coef_table, velocity_bins, slab_fracs, owners):
        _, freqs, rows, cols = wavefield.shape
        orders = coef_table.shape[2]
        steps = velocity_bins.shape[0]
        tiles = rows // 8 * (cols // LANES)
        chunks = min(n, tiles)
        chunk = (chunks, tiles // chunks * 8, LANES)
        fields = 2 * freqs
        ext_rows, ext_cols = rows + 2 * HALO, cols + LANES
        f32 = jnp.float32
        vmem = pl.BlockSpec(memory_space=pltpu.VMEM)
        hbm = pl.BlockSpec(memory_space=pltpu.HBM)
        dma = pltpu.SemaphoreType.DMA
        return pl.pallas_call(
            functools.partial(kernel, (n, n_tx, n_ty)),
            out_shape=(
                jax.ShapeDtypeStruct(wavefield.shape, f32),
                jax.ShapeDtypeStruct((steps, rows, cols), f32),
            ),
            in_specs=[pl.BlockSpec(memory_space=pltpu.SMEM), hbm, vmem, hbm, hbm],
            out_specs=(vmem, vmem),
            scratch_shapes=[
                pltpu.VMEM(velocity_bins.shape, jnp.int32),
                pltpu.VMEM(slab_fracs.shape, f32),
                pltpu.VMEM((steps, 2, freqs, rows, cols), f32),
                pltpu.VMEM((steps, 2, freqs, 2 * HALO, cols), f32),
                pltpu.VMEM((steps, rows, LANES), f32),
                pltpu.VMEM((steps, rows, LANES), f32),
                pltpu.VMEM((steps, ext_rows, LANES), f32),
                pltpu.VMEM((steps, ext_rows, LANES), f32),
                pltpu.VMEM((fields, ext_rows, LANES), f32),
                pltpu.VMEM((ext_rows, ext_cols), f32),
                pltpu.VMEM((orders, fields, ext_rows, ext_cols), f32),
                pltpu.VMEM((fields, 16, LANES), f32),
                pltpu.VMEM((fields, 16, LANES), f32),
                pltpu.VMEM((fields, orders, rows, cols), f32),
                pltpu.VMEM((fields, orders, rows, cols), f32),
                pltpu.VMEM((2, 1) + chunk, f32),
                pltpu.VMEM((2, steps - 1) + chunk, f32),
                pltpu.VMEM((2, n, 1) + chunk[1:], f32),
                pltpu.VMEM((2, n, steps - 1) + chunk[1:], f32),
                pltpu.VMEM((2, 1) + chunk, f32),
                pltpu.VMEM((2, steps - 1) + chunk, f32),
                dma((3,)),
                dma((steps, 3)),
                dma((steps, 3)),
                dma((4,)),
                dma((4,)),
                dma((4,)),
                dma((4,)),
            ],
            compiler_params=pltpu.CompilerParams(
                collective_id=0, has_side_effects=True, vmem_limit_bytes=60 * 1024 * 1024
            ),
        )(owners, wavefield, jnp.transpose(coef_table, (0, 2, 1, 3)), velocity_bins, slab_fracs)

    in_specs = (
        P(None, "freq", "tx", "ty"),
        P(None, "freq", None, None),
        P(None, "tx", "ty"),
        P("freq", "tx", "ty"),
        P(),
    )
    out_specs = (P(None, "freq", "tx", "ty"), P(None, "tx", "ty"))
    return jax.shard_map(on_device, mesh=mesh, in_specs=in_specs, out_specs=out_specs, check_vma=False)
```

```python
import functools
import math

import jax
import jax.numpy as jnp
from jax import lax
from jax.experimental import pallas as pl
from jax.experimental.pallas import tpu as pltpu
from jax.sharding import PartitionSpec as P

MESH = pl.DeviceIdType.MESH
LANES = 128
GROUP = 32
DEG = 8


def widths(steps):
    return [0] + [DEG * (steps - 1 - s) for s in range(1, steps)]


def kernel(sizes, outs, *refs):
    n, n_tx, n_ty = sizes
    refs = list(refs)

    def take(count):
        got = refs[:count]
        del refs[:count]
        return got

    owners, wave_hbm, table, bins_hbm, slabs_hbm, wave_out, images = take(7)
    bins, slabs = take(2)
    wv, lnd, pk_l, pk_r, in_r, in_l = (take(2) for _ in range(6))
    first, co_a, co_d = (take(len(outs)) for _ in range(3))
    tk, mask, tab_a, tab_d = take(4)
    bins_dn, bins_up, bins_r, bins_l, frac_dn, frac_up, frac_r, frac_l = take(8)
    src1, src3, land1, land3, dst1, dst3 = take(6)
    in_sem, halo_send, halo_recv, side_send, side_recv, rs_send, rs_recv, ag_send, ag_recv = take(9)

    me, tx, ty = lax.axis_index("freq"), lax.axis_index("tx"), lax.axis_index("ty")
    _, freqs, rows, cols = wave_hbm.shape
    steps = bins.shape[0]
    orders = table.shape[1]
    row_tiles, col_tiles = rows // 8, cols // LANES
    tiles = row_tiles * col_tiles
    chunks = min(n, tiles)
    per = tiles // chunks
    fields = 2 * freqs
    mine, group = lax.rem(me, chunks), lax.div(me, chunks) * chunks
    side = max(outs)
    side_tiles = side // 8
    wide = side_tiles > 0

    up, down = lax.rem(tx + n_tx - 1, n_tx), lax.rem(tx + 1, n_tx)
    left, right = lax.rem(ty + n_ty - 1, n_ty), lax.rem(ty + 1, n_ty)
    no_down = jnp.where(tx == n_tx - 1, 1, 0)
    no_up = jnp.where(tx == 0, 1, 0)
    no_right = jnp.where(ty == n_ty - 1, 1, 0)
    no_left = jnp.where(ty == 0, 1, 0)

    inputs = [
        pltpu.make_async_copy(slabs_hbm, slabs, in_sem.at[0]),
        pltpu.make_async_copy(wave_hbm, wv[0], in_sem.at[1]),
        pltpu.make_async_copy(bins_hbm, bins, in_sem.at[2]),
    ]
    for copy in inputs:
        copy.start()
    for e in range(2):
        lnd[e][...] = jnp.zeros_like(lnd[e])

    def there(x, y):
        return {"tx": x, "ty": y}

    def peer(d):
        return lax.rem(me + d, n)

    barrier = pltpu.get_barrier_semaphore()
    for d in range(1, n):
        pl.semaphore_signal(barrier, inc=1, device_id={"freq": peer(d)}, device_id_type=MESH)
    for x in (up, tx, down):
        for y in (left, ty, right):
            if x is not tx or y is not ty:
                pl.semaphore_signal(barrier, inc=1, device_id=there(x, y), device_id_type=MESH)

    def remote(src, dst, send, recv, to):
        return pltpu.make_async_remote_copy(
            src_ref=src, dst_ref=dst, send_sem=send, recv_sem=recv, device_id=to, device_id_type=MESH
        )

    def wait_for(ref, sem):
        pltpu.make_async_copy(ref, ref, sem).wait()

    def parts(g):
        if g in (0, 3):
            return src1.at[g // 3], land1.at[g // 3], dst1.at[g // 3]
        return src3.at[g - 1], land3.at[g - 1], dst3.at[g - 1]

    def chunk_at(ref, c):
        if per == 1:
            return ref.at[:, pl.ds(lax.div(c, col_tiles), 1), pl.ds(lax.rem(c, col_tiles), 1)]
        high = per // col_tiles
        return ref.at[:, pl.ds(c * high, high)]

    def scatter(g):
        src, land, _ = parts(g)
        for d in range(1, n):
            to = peer(d)
            remote(
                chunk_at(src, lax.rem(to, chunks)), land.at[d], rs_send.at[g], rs_recv.at[g], {"freq": to}
            ).start()

    def reduce_and_gather(g):
        src, land, dst = parts(g)
        wait_for(land.at[1:n], rs_recv.at[g])
        total = chunk_at(src, mine)[...]
        for d in range(1, n):
            total = total + land[d]
        here = chunk_at(dst, mine)
        here[...] = total
        for d in range(1, chunks):
            remote(here, here, ag_send.at[g], ag_recv.at[g], {"freq": group + lax.rem(mine + d, chunks)}).start()

    def gather_wait(g, sem):
        wait_for(parts(g)[1].at[1:chunks], sem.at[g])

    halo = [DEG + outs[0], DEG + outs[1]]

    def rows_up(e):
        w = halo[e]
        return remote(wv[e].at[:, :, 0:w], lnd[e].at[:, :, 0:w], halo_send.at[e, 0], halo_recv.at[e, 0], there(up, ty))

    def rows_down(e):
        w = halo[e]
        return remote(
            wv[e].at[:, :, rows - w : rows],
            lnd[e].at[:, :, w : 2 * w],
            halo_send.at[e, 1],
            halo_recv.at[e, 1],
            there(down, ty),
        )

    def columns(e):
        w = halo[e]
        copies = []
        for i, pk, landing, y in ((2, pk_l[e], in_r[e], left), (3, pk_r[e], in_l[e], right)):
            for src, dst, x in (
                (pk, landing.at[0:rows], tx),
                (pk.at[0:w], landing.at[rows : rows + w], up),
                (pk.at[rows - w : rows], landing.at[rows + w : rows + 2 * w], down),
            ):
                copies.append(remote(src, dst, halo_send.at[e, i], halo_recv.at[e, i], there(x, y)))
        return copies

    def send_halos(e):
        packed_l = packed_r = None
        lane = lax.broadcasted_iota(jnp.int32, (rows, LANES), 1)
        for i in range(fields):
            c, f = i // freqs, i % freqs
            start = wv[e][c, f, :, 0:LANES]
            end = wv[e][c, f, :, cols - LANES : cols]
            if i == 0:
                packed_l, packed_r = start, end
            else:
                packed_l = jnp.where(lane // GROUP == i, pltpu.roll(start, i * GROUP, 1), packed_l)
                packed_r = jnp.where(lane // GROUP == i - 1, pltpu.roll(end, i * GROUP, 1), packed_r)
        pk_l[e][...] = packed_l
        pk_r[e][...] = packed_r
        return lambda: start_halos(e)

    def start_halos(e):
        pl.when(tx > 0)(lambda: rows_up(e).start())
        pl.when(tx < n_tx - 1)(lambda: rows_down(e).start())
        for copy in columns(e):
            copy.start()

    def halo_recv_wait(e):
        pl.when(tx < n_tx - 1)(lambda: rows_up(e).wait_recv())
        pl.when(tx > 0)(lambda: rows_down(e).wait_recv())
        wait_for(in_r[e], halo_recv.at[e, 2])
        wait_for(in_l[e], halo_recv.at[e, 3])

    def halo_send_wait(e):
        pl.when(tx > 0)(lambda: rows_up(e).wait_send())
        pl.when(tx < n_tx - 1)(lambda: rows_down(e).wait_send())
        wait_for(in_r[e], halo_send.at[e, 2])
        wait_for(in_l[e], halo_send.at[e, 3])

    late = slice(1, steps - 1)

    def side_copies(g):
        if g == 0:
            pieces = [
                (0, bins.at[late, 0:side], bins_dn, up, ty),
                (1, bins.at[late, rows - side : rows], bins_up, down, ty),
            ]
            for i, landing, cs, y in (
                (2, bins_r, slice(0, LANES), left),
                (3, bins_l, slice(cols - LANES, cols), right),
            ):
                pieces += [
                    (i, bins.at[late, :, cs], landing.at[:, 0:rows], tx, y),
                    (i, bins.at[late, 0:side, cs], landing.at[:, rows : rows + side], up, y),
                    (i, bins.at[late, rows - side : rows, cs], landing.at[:, rows + side : rows + 2 * side], down, y),
                ]
        else:
            count, high = steps - 2, side_tiles
            src = dst3.at[0, 0:count]
            pieces = [
                (0, src.at[:, 0:high], frac_dn, up, ty),
                (1, src.at[:, row_tiles - high : row_tiles], frac_up, down, ty),
            ]
            for i, landing, ct, y in ((2, frac_r, 0, left), (3, frac_l, col_tiles - 1, right)):
                pieces += [
                    (i, src.at[:, :, ct], landing.at[:, 0:row_tiles], tx, y),
                    (i, src.at[:, 0:high, ct], landing.at[:, row_tiles : row_tiles + high], up, y),
                    (
                        i,
                        src.at[:, row_tiles - high : row_tiles, ct],
                        landing.at[:, row_tiles + high : row_tiles + 2 * high],
                        down,
                        y,
                    ),
                ]
        return [remote(a, b, side_send.at[g, i], side_recv.at[g, i], there(x, y)) for i, a, b, x, y in pieces]

    def side_wait(g, sem):
        for i, landing in enumerate(((bins_dn, bins_up, bins_r, bins_l), (frac_dn, frac_up, frac_r, frac_l))[g]):
            wait_for(landing, sem.at[g, i])

    def place(s, r):
        high = outs[s] // 8
        if r < row_tiles:
            return 0, r
        if r < row_tiles + high:
            return 1, r - row_tiles
        return 2, r - 2 * high

    def grid(s):
        high = outs[s] // 8
        return [
            (r, c) for r in range(row_tiles + 2 * high) for c in range(col_tiles + (1 if high else 0))
        ]

    lane8 = lax.broadcasted_iota(jnp.int32, (8, LANES), 1)

    def bins_tile(s, r, c):
        part, t = place(s, r)
        b = t - (row_tiles - side_tiles) if part == 2 else t
        if c < col_tiles:
            cs = slice(LANES * c, LANES * c + LANES)
            if part == 0:
                return bins[s, 8 * t : 8 * t + 8, cs]
            return (bins_dn, bins_up)[part - 1][s - 1, 8 * b : 8 * b + 8, cs]
        at = (0, rows, rows + side)[part] + 8 * b
        return jnp.where(lane8 < LANES // 2, bins_r[s - 1, at : at + 8], bins_l[s - 1, at : at + 8])

    def frac_tile(s, r, c):
        part, t = place(s, r)
        b = t - (row_tiles - side_tiles) if part == 2 else t
        if c < col_tiles:
            if part == 0:
                return dst1[0, 0, t, c] if s == 0 else dst3[0, s - 1, t, c]
            return (frac_dn, frac_up)[part - 1][s - 1, b, c]
        at = (0, row_tiles, row_tiles + side_tiles)[part] + b
        return jnp.where(lane8 < LANES // 2, frac_r[s - 1, at], frac_l[s - 1, at])

    inputs[0].wait()
    per_slab = slabs.shape[0]
    for j in range(steps):
        owner = owners[j]
        src = src1.at[0, 0] if j == 0 else src3.at[0, j - 1]
        for r in range(row_tiles):
            for c in range(col_tiles):
                value = jnp.zeros((8, LANES), jnp.float32)
                for i in range(per_slab):
                    tile = slabs[i, 8 * r : 8 * r + 8, LANES * c : LANES * c + LANES]
                    value = jnp.where(jnp.full((8, LANES), owner) == me * per_slab + i, tile, value)
                src[r, c] = value

    inputs[1].wait()
    send_halos(0)
    inputs[2].wait()
    pl.semaphore_wait(barrier, n - 1 + 8)
    scatter(0)
    start_halos(0)
    if wide:
        for copy in side_copies(0):
            copy.start()
    scatter(1)

    tab_a[...] = jnp.zeros_like(tab_a)
    for c in range(2):
        for f in range(freqs):
            tab_a[c * freqs + f, 0:orders, 0 : table.shape[3]] = table[c, :, f]
    for i in range(fields):
        tab_d[i] = pltpu.roll(tab_a[i], LANES - 1, 1) - tab_a[i]

    ext_cols = cols + LANES
    c = lax.broadcasted_iota(jnp.int32, (8, ext_cols), 1)
    beside = jnp.where(c >= cols + LANES // 2, no_left, jnp.where(c >= cols, no_right, 0))
    for i, no_row in enumerate((0, no_down, no_up)):
        mask[i] = jnp.where(beside + no_row > 0, 0.0, 0.25)

    def quarter(w):
        high = w // 8
        return jnp.concatenate([mask[0]] * row_tiles + [mask[1]] * high + [mask[2]] * high, axis=0)

    def lookup(s):
        def one(i, carry):
            for r, c in grid(s):
                rs, cs = slice(8 * r, 8 * r + 8), slice(LANES * c, LANES * c + LANES)
                index = bins_tile(s, r, c)
                for k in range(orders):
                    for tab, co in ((tab_a, co_a[s]), (tab_d, co_d[s])):
                        row = jnp.broadcast_to(tab[i, k : k + 1, :], (8, LANES))
                        co[i, k, rs, cs] = jnp.take_along_axis(row, index, axis=1, mode="promise_in_bounds")
            return carry

        lax.fori_loop(0, fields, one, 0)

    def unpack(e):
        w = halo[e]
        ext = rows + 2 * w
        lane = lax.broadcasted_iota(jnp.int32, (ext, LANES), 1)
        one_roll = 2 * w <= GROUP
        if one_roll:
            both = jnp.where(lax.rem(lane, GROUP) < GROUP // 2, in_r[e][...], in_l[e][...])
        for i in range(fields):
            by = (LANES - i * GROUP) % LANES
            turn = (lambda v: pltpu.roll(v, by, 1)) if by else (lambda v: v)
            if one_roll:
                beyond = turn(both)
            else:
                beyond = jnp.where(lane < LANES // 2, turn(in_r[e][...]), turn(in_l[e][...]))
            own = jnp.concatenate([wv[e][i // freqs, i % freqs], lnd[e][i // freqs, i % freqs]], axis=0)
            t = jnp.concatenate([own, beyond], axis=1)
            first[e][i] = jnp.where(quarter(w) > 0.0, t, 0.0)

    def recurrence(s):
        w = outs[s] + DEG
        ext = rows + 2 * w

        def term(k, i):
            return first[s][i] if k == 0 else tk[k - 1, i, 0:ext]

        for k in range(1, orders):
            twice, summed, moved = [], [], []
            for i in range(fields):
                t = term(k - 1, i)
                twice.append(t + t)
                summed.append(twice[i] + (pltpu.roll(t, 1, 0) + pltpu.roll(t, ext - 1, 0)))
            for i in range(fields):
                moved.append(pltpu.roll(summed[i], 1, 1) + pltpu.roll(summed[i], ext_cols - 1, 1))
            for i in range(fields):
                smooth = (summed[i] + summed[i] + moved[i]) * quarter(w)
                if k == 1:
                    tk[0, i, 0:ext] = 0.5 * (smooth - twice[i])
                else:
                    tk[k - 1, i, 0:ext] = (smooth - term(k - 2, i)) - twice[i]

    scale = 1.0 / math.sqrt(freqs * n)

    def combine(s):
        image = src1.at[1, 0] if s == steps - 1 else src3.at[1, s]
        for r, c in grid(s):
            rs, cs = slice(8 * r, 8 * r + 8), slice(LANES * c, LANES * c + LANES)
            part, t = place(s, r)
            at = 8 * r if part < 2 else 8 * r + 2 * DEG
            ts = slice(at, at + 8)
            fraction = frac_tile(s, r, c)
            summed = None
            for f in range(freqs):
                re = im = None
                for k in range(orders):
                    t_re = first[s][f, ts, cs] if k == 0 else tk[k - 1, f, ts, cs]
                    t_im = first[s][freqs + f, ts, cs] if k == 0 else tk[k - 1, freqs + f, ts, cs]
                    c_re = co_a[s][f, k, rs, cs] + fraction * co_d[s][f, k, rs, cs]
                    c_im = co_a[s][freqs + f, k, rs, cs] + fraction * co_d[s][freqs + f, k, rs, cs]
                    add_re = c_re * t_re - c_im * t_im
                    add_im = c_re * t_im + c_im * t_re
                    re = add_re if k == 0 else re + add_re
                    im = add_im if k == 0 else im + add_im
                if s == steps - 1:
                    wave_out[0, f, rs, cs] = re
                    wave_out[1, f, rs, cs] = im
                elif s == 0:
                    wv[1][0, f, rs, cs] = re
                    wv[1][1, f, rs, cs] = im
                else:
                    first[s + 1][f, rs, cs] = re
                    first[s + 1][freqs + f, rs, cs] = im
                summed = re if f == 0 else summed + re
            if part == 0 and c < col_tiles:
                image[t, c] = summed * scale

    lookup(0)
    reduce_and_gather(0)
    halo_recv_wait(0)
    unpack(0)
    recurrence(0)
    reduce_and_gather(1)
    gather_wait(0, ag_recv)
    combine(0)
    send_halos(1)
    start_halos(1)
    if wide:
        side_wait(0, side_recv)
    lookup(1)
    gather_wait(1, ag_recv)
    if wide:
        for copy in side_copies(1):
            copy.start()
    for s in range(2, steps):
        lookup(s)
    halo_recv_wait(1)
    unpack(1)
    for s in range(1, steps):
        recurrence(s)
        if s == 1 and wide:
            side_wait(1, side_recv)
        combine(s)
        if s == steps - 2:
            scatter(2)
    scatter(3)
    reduce_and_gather(2)
    reduce_and_gather(3)

    def put_image(j, src):
        for r in range(row_tiles):
            for c in range(col_tiles):
                images[j, 8 * r : 8 * r + 8, LANES * c : LANES * c + LANES] = src[r, c]

    gather_wait(2, ag_recv)
    for j in range(steps - 1):
        put_image(j, dst3.at[1, j])
    for e in range(2):
        halo_send_wait(e)
        if wide:
            side_wait(e, side_send)
    for g in range(4):
        wait_for(parts(g)[1].at[1:n], rs_send.at[g])
    for g in range(3):
        gather_wait(g, ag_send)
    gather_wait(3, ag_recv)
    put_image(steps - 1, dst1.at[1, 0])
    gather_wait(3, ag_send)


def solution(mesh):
    n, n_tx, n_ty = (mesh.shape[axis] for axis in ("freq", "tx", "ty"))

    def on_device(wavefield, coef_table, velocity_bins, slab_fracs, owners):
        _, freqs, rows, cols = wavefield.shape
        orders = coef_table.shape[2]
        steps = velocity_bins.shape[0]
        row_tiles, col_tiles = rows // 8, cols // LANES
        tiles = row_tiles * col_tiles
        per = tiles // min(n, tiles)
        chunk = (per // col_tiles, col_tiles) if per > 1 else (1, 1)
        outs = widths(steps)
        side = max(outs)
        fields = 2 * freqs
        ext_cols = cols + LANES
        f32, i32 = jnp.float32, jnp.int32
        vmem = pl.BlockSpec(memory_space=pltpu.VMEM)
        hbm = pl.BlockSpec(memory_space=pltpu.HBM)
        dma = pltpu.SemaphoreType.DMA
        tile = (8, LANES)

        def ext(s):
            return rows + 2 * (outs[s] + DEG)

        coefs = [
            pltpu.VMEM((fields, orders, rows + 2 * w, cols + (LANES if w else 0)), f32) for w in outs
        ]
        scratch = [pltpu.VMEM(velocity_bins.shape, i32), pltpu.VMEM(slab_fracs.shape, f32)]
        scratch += [pltpu.VMEM((2, freqs, rows, cols), f32) for e in range(2)]
        scratch += [pltpu.VMEM((2, freqs, ext(e) - rows, cols), f32) for e in range(2)]
        scratch += [pltpu.VMEM((rows, LANES), f32) for _ in range(4)]
        scratch += [pltpu.VMEM((ext(e), LANES), f32) for e in (0, 1, 0, 1)]
        scratch += [pltpu.VMEM((fields, ext(s), ext_cols), f32) for s in range(steps)]
        scratch += coefs + coefs
        scratch += [
            pltpu.VMEM((orders - 1, fields, max(map(ext, range(steps))), ext_cols), f32),
            pltpu.VMEM((3, 8, ext_cols), f32),
            pltpu.VMEM((fields, 16, LANES), f32),
            pltpu.VMEM((fields, 16, LANES), f32),
        ]
        late, high = steps - 2, side // 8
        scratch += [pltpu.VMEM((late, side, cols), i32) for _ in range(2)]
        scratch += [pltpu.VMEM((late, rows + 2 * side, LANES), i32) for _ in range(2)]
        scratch += [pltpu.VMEM((late, high, col_tiles) + tile, f32) for _ in range(2)]
        scratch += [pltpu.VMEM((late, row_tiles + 2 * high) + tile, f32) for _ in range(2)]
        for lead in ((), (n,), ()):
            shape = (chunk if lead else (row_tiles, col_tiles)) + tile
            scratch += [pltpu.VMEM((2,) + lead + (m,) + shape, f32) for m in (1, steps - 1)]
        scratch += [dma((3,)), dma((2, 4)), dma((2, 4)), dma((2, 4)), dma((2, 4))]
        scratch += [dma((4,)) for _ in range(4)]
        return pl.pallas_call(
            functools.partial(kernel, (n, n_tx, n_ty), outs),
            out_shape=(
                jax.ShapeDtypeStruct(wavefield.shape, f32),
                jax.ShapeDtypeStruct((steps, rows, cols), f32),
            ),
            in_specs=[pl.BlockSpec(memory_space=pltpu.SMEM), hbm, vmem, hbm, hbm],
            out_specs=(vmem, vmem),
            scratch_shapes=scratch,
            compiler_params=pltpu.CompilerParams(
                collective_id=0, has_side_effects=True, vmem_limit_bytes=60 * 1024 * 1024
            ),
        )(owners, wavefield, jnp.transpose(coef_table, (0, 2, 1, 3)), velocity_bins, slab_fracs)

    in_specs = (
        P(None, "freq", "tx", "ty"),
        P(None, "freq", None, None),
        P(None, "tx", "ty"),
        P("freq", "tx", "ty"),
        P(),
    )
    out_specs = (P(None, "freq", "tx", "ty"), P(None, "tx", "ty"))
    return jax.shard_map(on_device, mesh=mesh, in_specs=in_specs, out_specs=out_specs, check_vma=False)
```

```python
import functools
import math

import jax
import jax.numpy as jnp
from jax import lax
from jax.experimental import pallas as pl
from jax.experimental.pallas import tpu as pltpu
from jax.sharding import PartitionSpec as P

MESH = pl.DeviceIdType.MESH
LANES = 128
GROUP = 32
DEG = 8


def widths(steps):
    return [0] + [DEG * (steps - 1 - s) for s in range(1, steps)]


def kernel(sizes, outs, *refs):
    n, n_tx, n_ty = sizes
    refs = list(refs)

    def take(count):
        got = refs[:count]
        del refs[:count]
        return got

    owners, wave_hbm, table, bins_hbm, slabs_hbm, wave_out, images = take(7)
    bins, slabs = take(2)
    wv, lnd, pk_l, pk_r, in_r, in_l = (take(2) for _ in range(6))
    first, co_a, co_d = (take(len(outs)) for _ in range(3))
    tk, mask, tab_a, tab_d = take(4)
    bins_dn, bins_up, bins_r, bins_l, frac_dn, frac_up, frac_r, frac_l = take(8)
    src, land, dst = take(5), take(5), take(5)
    in_sem, halo_send, halo_recv, side_send, side_recv, rs_send, rs_recv, ag_send, ag_recv = take(9)

    me, tx, ty = lax.axis_index("freq"), lax.axis_index("tx"), lax.axis_index("ty")
    _, freqs, rows, cols = wave_hbm.shape
    steps = bins.shape[0]
    orders = table.shape[1]
    row_tiles, col_tiles = rows // 8, cols // LANES
    tiles = row_tiles * col_tiles
    chunks = min(n, tiles)
    per = tiles // chunks
    fields = 2 * freqs
    mine, group = lax.rem(me, chunks), lax.div(me, chunks) * chunks
    side = max(outs)
    side_tiles = side // 8
    wide = side_tiles > 0

    up, down = lax.rem(tx + n_tx - 1, n_tx), lax.rem(tx + 1, n_tx)
    left, right = lax.rem(ty + n_ty - 1, n_ty), lax.rem(ty + 1, n_ty)
    no_down = jnp.where(tx == n_tx - 1, 1, 0)
    no_up = jnp.where(tx == 0, 1, 0)
    no_right = jnp.where(ty == n_ty - 1, 1, 0)
    no_left = jnp.where(ty == 0, 1, 0)

    inputs = [
        pltpu.make_async_copy(slabs_hbm, slabs, in_sem.at[0]),
        pltpu.make_async_copy(wave_hbm, wv[0], in_sem.at[1]),
        pltpu.make_async_copy(bins_hbm, bins, in_sem.at[2]),
    ]
    for copy in inputs:
        copy.start()
    for e in range(2):
        lnd[e][...] = jnp.zeros_like(lnd[e])

    def there(x, y):
        return {"tx": x, "ty": y}

    def peer(d):
        return lax.rem(me + d, n)

    barrier = pltpu.get_barrier_semaphore()
    for d in range(1, n):
        pl.semaphore_signal(barrier, inc=1, device_id={"freq": peer(d)}, device_id_type=MESH)
    for x in (up, tx, down):
        for y in (left, ty, right):
            if x is not tx or y is not ty:
                pl.semaphore_signal(barrier, inc=1, device_id=there(x, y), device_id_type=MESH)

    def remote(src, dst, send, recv, to):
        return pltpu.make_async_remote_copy(
            src_ref=src, dst_ref=dst, send_sem=send, recv_sem=recv, device_id=to, device_id_type=MESH
        )

    def wait_for(ref, sem):
        pltpu.make_async_copy(ref, ref, sem).wait()

    def chunk_at(ref, c):
        if per == 1:
            return ref.at[:, pl.ds(lax.div(c, col_tiles), 1), pl.ds(lax.rem(c, col_tiles), 1)]
        high = per // col_tiles
        return ref.at[:, pl.ds(c * high, high)]

    def scatter(g):
        for d in range(1, n):
            to = peer(d)
            remote(
                chunk_at(src[g], lax.rem(to, chunks)), land[g].at[d], rs_send.at[g], rs_recv.at[g], {"freq": to}
            ).start()

    def reduce_and_gather(g):
        wait_for(land[g].at[1:n], rs_recv.at[g])
        total = chunk_at(src[g], mine)[...]
        for d in range(1, n):
            total = total + land[g][d]
        here = chunk_at(dst[g], mine)
        here[...] = total
        for d in range(1, chunks):
            remote(here, here, ag_send.at[g], ag_recv.at[g], {"freq": group + lax.rem(mine + d, chunks)}).start()

    def gather_wait(g, sem):
        wait_for(land[g].at[1:chunks], sem.at[g])

    halo = [DEG + outs[0], DEG + outs[1]]

    def rows_up(e):
        w = halo[e]
        return remote(wv[e].at[:, :, 0:w], lnd[e].at[:, :, 0:w], halo_send.at[e, 0], halo_recv.at[e, 0], there(up, ty))

    def rows_down(e):
        w = halo[e]
        return remote(
            wv[e].at[:, :, rows - w : rows],
            lnd[e].at[:, :, w : 2 * w],
            halo_send.at[e, 1],
            halo_recv.at[e, 1],
            there(down, ty),
        )

    def columns(e):
        w = halo[e]
        copies = []
        for i, pk, landing, y in ((2, pk_l[e], in_r[e], left), (3, pk_r[e], in_l[e], right)):
            for src, dst, x in (
                (pk, landing.at[0:rows], tx),
                (pk.at[0:w], landing.at[rows : rows + w], up),
                (pk.at[rows - w : rows], landing.at[rows + w : rows + 2 * w], down),
            ):
                copies.append(remote(src, dst, halo_send.at[e, i], halo_recv.at[e, i], there(x, y)))
        return copies

    def send_halos(e):
        packed_l = packed_r = None
        lane = lax.broadcasted_iota(jnp.int32, (rows, LANES), 1)
        for i in range(fields):
            c, f = i // freqs, i % freqs
            start = wv[e][c, f, :, 0:LANES]
            end = wv[e][c, f, :, cols - LANES : cols]
            if i == 0:
                packed_l, packed_r = start, end
            else:
                packed_l = jnp.where(lane // GROUP == i, pltpu.roll(start, i * GROUP, 1), packed_l)
                packed_r = jnp.where(lane // GROUP == i - 1, pltpu.roll(end, i * GROUP, 1), packed_r)
        pk_l[e][...] = packed_l
        pk_r[e][...] = packed_r
        return lambda: start_halos(e)

    def start_halos(e):
        pl.when(tx > 0)(lambda: rows_up(e).start())
        pl.when(tx < n_tx - 1)(lambda: rows_down(e).start())
        for copy in columns(e):
            copy.start()

    def halo_recv_wait(e):
        pl.when(tx < n_tx - 1)(lambda: rows_up(e).wait_recv())
        pl.when(tx > 0)(lambda: rows_down(e).wait_recv())
        wait_for(in_r[e], halo_recv.at[e, 2])
        wait_for(in_l[e], halo_recv.at[e, 3])

    def halo_send_wait(e):
        pl.when(tx > 0)(lambda: rows_up(e).wait_send())
        pl.when(tx < n_tx - 1)(lambda: rows_down(e).wait_send())
        wait_for(in_r[e], halo_send.at[e, 2])
        wait_for(in_l[e], halo_send.at[e, 3])

    late = slice(1, steps - 1)

    def side_copies(g):
        if g == 0:
            pieces = [
                (0, bins.at[late, 0:side], bins_dn, up, ty),
                (1, bins.at[late, rows - side : rows], bins_up, down, ty),
            ]
            for i, landing, cs, y in (
                (2, bins_r, slice(0, LANES), left),
                (3, bins_l, slice(cols - LANES, cols), right),
            ):
                pieces += [
                    (i, bins.at[late, :, cs], landing.at[:, 0:rows], tx, y),
                    (i, bins.at[late, 0:side, cs], landing.at[:, rows : rows + side], up, y),
                    (i, bins.at[late, rows - side : rows, cs], landing.at[:, rows + side : rows + 2 * side], down, y),
                ]
        else:
            count, high = steps - 2, side_tiles
            cut = dst[1].at[0:count]
            pieces = [
                (0, cut.at[:, 0:high], frac_dn, up, ty),
                (1, cut.at[:, row_tiles - high : row_tiles], frac_up, down, ty),
            ]
            for i, landing, ct, y in ((2, frac_r, 0, left), (3, frac_l, col_tiles - 1, right)):
                pieces += [
                    (i, cut.at[:, :, ct], landing.at[:, 0:row_tiles], tx, y),
                    (i, cut.at[:, 0:high, ct], landing.at[:, row_tiles : row_tiles + high], up, y),
                    (
                        i,
                        cut.at[:, row_tiles - high : row_tiles, ct],
                        landing.at[:, row_tiles + high : row_tiles + 2 * high],
                        down,
                        y,
                    ),
                ]
        return [remote(a, b, side_send.at[g, i], side_recv.at[g, i], there(x, y)) for i, a, b, x, y in pieces]

    def side_wait(g, sem):
        for i, landing in enumerate(((bins_dn, bins_up, bins_r, bins_l), (frac_dn, frac_up, frac_r, frac_l))[g]):
            wait_for(landing, sem.at[g, i])

    def place(s, r):
        high = outs[s] // 8
        if r < row_tiles:
            return 0, r
        if r < row_tiles + high:
            return 1, r - row_tiles
        return 2, r - 2 * high

    def grid(s):
        high = outs[s] // 8
        return [
            (r, c) for r in range(row_tiles + 2 * high) for c in range(col_tiles + (1 if high else 0))
        ]

    lane8 = lax.broadcasted_iota(jnp.int32, (8, LANES), 1)

    def bins_tile(s, r, c):
        part, t = place(s, r)
        b = t - (row_tiles - side_tiles) if part == 2 else t
        if c < col_tiles:
            cs = slice(LANES * c, LANES * c + LANES)
            if part == 0:
                return bins[s, 8 * t : 8 * t + 8, cs]
            return (bins_dn, bins_up)[part - 1][s - 1, 8 * b : 8 * b + 8, cs]
        at = (0, rows, rows + side)[part] + 8 * b
        return jnp.where(lane8 < LANES // 2, bins_r[s - 1, at : at + 8], bins_l[s - 1, at : at + 8])

    def frac_tile(s, r, c):
        part, t = place(s, r)
        b = t - (row_tiles - side_tiles) if part == 2 else t
        if c < col_tiles:
            if part == 0:
                return dst[0][0, t, c] if s == 0 else dst[1][s - 1, t, c]
            return (frac_dn, frac_up)[part - 1][s - 1, b, c]
        at = (0, row_tiles, row_tiles + side_tiles)[part] + b
        return jnp.where(lane8 < LANES // 2, frac_r[s - 1, at], frac_l[s - 1, at])

    inputs[0].wait()
    per_slab = slabs.shape[0]
    for j in range(steps):
        owner = owners[j]
        chosen = src[0].at[0] if j == 0 else src[1].at[j - 1]
        for r in range(row_tiles):
            for c in range(col_tiles):
                value = jnp.zeros((8, LANES), jnp.float32)
                for i in range(per_slab):
                    tile = slabs[i, 8 * r : 8 * r + 8, LANES * c : LANES * c + LANES]
                    value = jnp.where(jnp.full((8, LANES), owner) == me * per_slab + i, tile, value)
                chosen[r, c] = value

    inputs[1].wait()
    send_halos(0)
    inputs[2].wait()
    pl.semaphore_wait(barrier, n - 1 + 8)
    scatter(0)
    start_halos(0)
    if wide:
        for copy in side_copies(0):
            copy.start()

    tab_a[...] = jnp.zeros_like(tab_a)
    for c in range(2):
        for f in range(freqs):
            tab_a[c * freqs + f, 0:orders, 0 : table.shape[3]] = table[c, :, f]
    for i in range(fields):
        tab_d[i] = pltpu.roll(tab_a[i], LANES - 1, 1) - tab_a[i]

    ext_cols = cols + LANES
    c = lax.broadcasted_iota(jnp.int32, (8, ext_cols), 1)
    beside = jnp.where(c >= cols + LANES // 2, no_left, jnp.where(c >= cols, no_right, 0))
    for i, no_row in enumerate((0, no_down, no_up)):
        mask[i] = jnp.where(beside + no_row > 0, 0.0, 0.25)

    def quarter(w):
        high = w // 8
        return jnp.concatenate([mask[0]] * row_tiles + [mask[1]] * high + [mask[2]] * high, axis=0)

    def lookup(s):
        def one(i, carry):
            for r, c in grid(s):
                rs, cs = slice(8 * r, 8 * r + 8), slice(LANES * c, LANES * c + LANES)
                index = bins_tile(s, r, c)
                for k in range(orders):
                    for tab, co in ((tab_a, co_a[s]), (tab_d, co_d[s])):
                        row = jnp.broadcast_to(tab[i, k : k + 1, :], (8, LANES))
                        co[i, k, rs, cs] = jnp.take_along_axis(row, index, axis=1, mode="promise_in_bounds")
            return carry

        lax.fori_loop(0, fields, one, 0)

    def unpack(e):
        w = halo[e]
        ext = rows + 2 * w
        lane = lax.broadcasted_iota(jnp.int32, (ext, LANES), 1)
        one_roll = 2 * w <= GROUP
        if one_roll:
            both = jnp.where(lax.rem(lane, GROUP) < GROUP // 2, in_r[e][...], in_l[e][...])
        for i in range(fields):
            by = (LANES - i * GROUP) % LANES
            turn = (lambda v: pltpu.roll(v, by, 1)) if by else (lambda v: v)
            if one_roll:
                beyond = turn(both)
            else:
                beyond = jnp.where(lane < LANES // 2, turn(in_r[e][...]), turn(in_l[e][...]))
            own = jnp.concatenate([wv[e][i // freqs, i % freqs], lnd[e][i // freqs, i % freqs]], axis=0)
            t = jnp.concatenate([own, beyond], axis=1)
            first[e][i] = jnp.where(quarter(w) > 0.0, t, 0.0)

    def recurrence(s):
        w = outs[s] + DEG
        ext = rows + 2 * w

        def term(k, i):
            return first[s][i] if k == 0 else tk[k - 1, i, 0:ext]

        for k in range(1, orders):
            twice, summed, moved = [], [], []
            for i in range(fields):
                t = term(k - 1, i)
                twice.append(t + t)
                summed.append(twice[i] + (pltpu.roll(t, 1, 0) + pltpu.roll(t, ext - 1, 0)))
            for i in range(fields):
                moved.append(pltpu.roll(summed[i], 1, 1) + pltpu.roll(summed[i], ext_cols - 1, 1))
            for i in range(fields):
                smooth = (summed[i] + summed[i] + moved[i]) * quarter(w)
                if k == 1:
                    tk[0, i, 0:ext] = 0.5 * (smooth - twice[i])
                else:
                    tk[k - 1, i, 0:ext] = (smooth - term(k - 2, i)) - twice[i]

    def image_at(s):
        return (2, 0) if s == 0 else (4, 0) if s == steps - 1 else (3, s - 1)

    scale = 1.0 / math.sqrt(freqs * n)

    def combine(s):
        g, j = image_at(s)
        image = src[g].at[j]
        for r, c in grid(s):
            rs, cs = slice(8 * r, 8 * r + 8), slice(LANES * c, LANES * c + LANES)
            part, t = place(s, r)
            at = 8 * r if part < 2 else 8 * r + 2 * DEG
            ts = slice(at, at + 8)
            fraction = frac_tile(s, r, c)
            summed = None
            for f in range(freqs):
                re = im = None
                for k in range(orders):
                    t_re = first[s][f, ts, cs] if k == 0 else tk[k - 1, f, ts, cs]
                    t_im = first[s][freqs + f, ts, cs] if k == 0 else tk[k - 1, freqs + f, ts, cs]
                    c_re = co_a[s][f, k, rs, cs] + fraction * co_d[s][f, k, rs, cs]
                    c_im = co_a[s][freqs + f, k, rs, cs] + fraction * co_d[s][freqs + f, k, rs, cs]
                    add_re = c_re * t_re - c_im * t_im
                    add_im = c_re * t_im + c_im * t_re
                    re = add_re if k == 0 else re + add_re
                    im = add_im if k == 0 else im + add_im
                if s == steps - 1:
                    wave_out[0, f, rs, cs] = re
                    wave_out[1, f, rs, cs] = im
                elif s == 0:
                    wv[1][0, f, rs, cs] = re
                    wv[1][1, f, rs, cs] = im
                else:
                    first[s + 1][f, rs, cs] = re
                    first[s + 1][freqs + f, rs, cs] = im
                summed = re if f == 0 else summed + re
            if part == 0 and c < col_tiles:
                image[t, c] = summed * scale

    lookup(0)
    for s in range(steps - 1, 1, -1):
        if s == steps - 2 and wide:
            side_wait(0, side_recv)
        lookup(s)
    reduce_and_gather(0)
    scatter(1)
    halo_recv_wait(0)
    unpack(0)
    recurrence(0)
    gather_wait(0, ag_recv)
    combine(0)
    send_halos(1)
    start_halos(1)
    reduce_and_gather(1)
    lookup(1)
    gather_wait(1, ag_recv)
    if wide:
        for copy in side_copies(1):
            copy.start()
    scatter(2)
    halo_recv_wait(1)
    unpack(1)
    for s in range(1, steps):
        recurrence(s)
        if s == 1 and wide:
            side_wait(1, side_recv)
        combine(s)
        if s == steps - 2:
            scatter(3)
    scatter(4)
    for g in range(2, 5):
        reduce_and_gather(g)

    def put_image(s):
        g, j = image_at(s)
        for r in range(row_tiles):
            for c in range(col_tiles):
                images[s, 8 * r : 8 * r + 8, LANES * c : LANES * c + LANES] = dst[g][j, r, c]

    for g in range(2, 4):
        gather_wait(g, ag_recv)
    for s in range(steps - 1):
        put_image(s)
    for e in range(2):
        halo_send_wait(e)
        if wide:
            side_wait(e, side_send)
    for g in range(5):
        wait_for(land[g].at[1:n], rs_send.at[g])
    for g in range(4):
        gather_wait(g, ag_send)
    gather_wait(4, ag_recv)
    put_image(steps - 1)
    gather_wait(4, ag_send)


def settle(wave, image, wave_out, images, sem):
    copies = [pltpu.make_async_copy(wave, wave_out, sem.at[0]), pltpu.make_async_copy(image, images, sem.at[1])]
    for copy in copies:
        copy.start()
    for copy in copies:
        copy.wait()


def solution(mesh):
    n, n_tx, n_ty = (mesh.shape[axis] for axis in ("freq", "tx", "ty"))

    def on_device(wavefield, coef_table, velocity_bins, slab_fracs, owners):
        _, freqs, rows, cols = wavefield.shape
        orders = coef_table.shape[2]
        steps = velocity_bins.shape[0]
        row_tiles, col_tiles = rows // 8, cols // LANES
        tiles = row_tiles * col_tiles
        per = tiles // min(n, tiles)
        chunk = (per // col_tiles, col_tiles) if per > 1 else (1, 1)
        outs = widths(steps)
        side = max(outs)
        fields = 2 * freqs
        ext_cols = cols + LANES
        f32, i32 = jnp.float32, jnp.int32
        vmem = pl.BlockSpec(memory_space=pltpu.VMEM)
        hbm = pl.BlockSpec(memory_space=pltpu.HBM)
        dma = pltpu.SemaphoreType.DMA
        tile = (8, LANES)

        def ext(s):
            return rows + 2 * (outs[s] + DEG)

        coefs = [
            pltpu.VMEM((fields, orders, rows + 2 * w, cols + (LANES if w else 0)), f32) for w in outs
        ]
        scratch = [pltpu.VMEM(velocity_bins.shape, i32), pltpu.VMEM(slab_fracs.shape, f32)]
        scratch += [pltpu.VMEM((2, freqs, rows, cols), f32) for e in range(2)]
        scratch += [pltpu.VMEM((2, freqs, ext(e) - rows, cols), f32) for e in range(2)]
        scratch += [pltpu.VMEM((rows, LANES), f32) for _ in range(4)]
        scratch += [pltpu.VMEM((ext(e), LANES), f32) for e in (0, 1, 0, 1)]
        scratch += [pltpu.VMEM((fields, ext(s), ext_cols), f32) for s in range(steps)]
        scratch += coefs + coefs
        scratch += [
            pltpu.VMEM((orders - 1, fields, max(map(ext, range(steps))), ext_cols), f32),
            pltpu.VMEM((3, 8, ext_cols), f32),
            pltpu.VMEM((fields, 16, LANES), f32),
            pltpu.VMEM((fields, 16, LANES), f32),
        ]
        late, high = steps - 2, side // 8
        scratch += [pltpu.VMEM((late, side, cols), i32) for _ in range(2)]
        scratch += [pltpu.VMEM((late, rows + 2 * side, LANES), i32) for _ in range(2)]
        scratch += [pltpu.VMEM((late, high, col_tiles) + tile, f32) for _ in range(2)]
        scratch += [pltpu.VMEM((late, row_tiles + 2 * high) + tile, f32) for _ in range(2)]
        for lead in ((), (n,), ()):
            shape = (chunk if lead else (row_tiles, col_tiles)) + tile
            scratch += [pltpu.VMEM(lead + (m,) + shape, f32) for m in (1, steps - 1, 1, steps - 2, 1)]
        scratch += [dma((3,)), dma((2, 4)), dma((2, 4)), dma((2, 4)), dma((2, 4))]
        scratch += [dma((5,)) for _ in range(4)]
        results = pl.pallas_call(
            functools.partial(kernel, (n, n_tx, n_ty), outs),
            out_shape=(
                jax.ShapeDtypeStruct(wavefield.shape, f32),
                jax.ShapeDtypeStruct((steps, rows, cols), f32),
            ),
            in_specs=[pl.BlockSpec(memory_space=pltpu.SMEM), hbm, vmem, hbm, hbm],
            out_specs=(vmem, vmem),
            scratch_shapes=scratch,
            compiler_params=pltpu.CompilerParams(
                collective_id=0, has_side_effects=True, vmem_limit_bytes=60 * 1024 * 1024
            ),
        )(owners, wavefield, jnp.transpose(coef_table, (0, 2, 1, 3)), velocity_bins, slab_fracs)
        return pl.pallas_call(
            settle,
            out_shape=tuple(jax.ShapeDtypeStruct(x.shape, f32) for x in results),
            in_specs=[hbm, hbm],
            out_specs=(hbm, hbm),
            scratch_shapes=[dma((2,))],
            compiler_params=pltpu.CompilerParams(vmem_limit_bytes=60 * 1024 * 1024),
        )(*results)

    in_specs = (
        P(None, "freq", "tx", "ty"),
        P(None, "freq", None, None),
        P(None, "tx", "ty"),
        P("freq", "tx", "ty"),
        P(),
    )
    out_specs = (P(None, "freq", "tx", "ty"), P(None, "tx", "ty"))
    return jax.shard_map(on_device, mesh=mesh, in_specs=in_specs, out_specs=out_specs, check_vma=False)
```

```python
import functools
import math

import jax
import jax.numpy as jnp
from jax import lax
from jax.experimental import pallas as pl
from jax.experimental.pallas import tpu as pltpu
from jax.sharding import PartitionSpec as P

MESH = pl.DeviceIdType.MESH
LANES = 128
GROUP = 32
DEG = 8


def widths(steps):
    return [0] * (steps - 2) + [DEG, 0]


def kernel(sizes, outs, *refs):
    n, n_tx, n_ty = sizes
    refs = list(refs)

    def take(count):
        got = refs[:count]
        del refs[:count]
        return got

    owners, wave_hbm, table_hbm, bins_hbm, slabs_hbm, wave_out, images = take(7)
    table, bins, slabs = take(3)
    wv, lnd, pk_l, pk_r, in_r, in_l = (take(len(outs) - 1) for _ in range(6))
    first, co_a, co_d = (take(len(outs)) for _ in range(3))
    tk, mask, tab_a, tab_d = take(4)
    bins_dn, bins_up, bins_r, bins_l, frac_dn, frac_up, frac_r, frac_l = take(8)
    src, land, dst = take(5), take(5), take(5)
    in_sem, halo_send, halo_recv, side_send, side_recv, rs_send, rs_recv, ag_send, ag_recv = take(9)

    me, tx, ty = lax.axis_index("freq"), lax.axis_index("tx"), lax.axis_index("ty")
    _, freqs, rows, cols = wave_hbm.shape
    steps = bins.shape[0]
    orders = table.shape[1]
    row_tiles, col_tiles = rows // 8, cols // LANES
    tiles = row_tiles * col_tiles
    chunks = min(n, tiles)
    per = tiles // chunks
    fields = 2 * freqs
    mine, group = lax.rem(me, chunks), lax.div(me, chunks) * chunks
    side = max(outs)
    side_tiles = side // 8

    up, down = lax.rem(tx + n_tx - 1, n_tx), lax.rem(tx + 1, n_tx)
    left, right = lax.rem(ty + n_ty - 1, n_ty), lax.rem(ty + 1, n_ty)
    no_down = jnp.where(tx == n_tx - 1, 1, 0)
    no_up = jnp.where(tx == 0, 1, 0)
    no_right = jnp.where(ty == n_ty - 1, 1, 0)
    no_left = jnp.where(ty == 0, 1, 0)

    inputs = [
        pltpu.make_async_copy(slabs_hbm, slabs, in_sem.at[0]),
        pltpu.make_async_copy(wave_hbm, wv[0], in_sem.at[1]),
        pltpu.make_async_copy(bins_hbm, bins, in_sem.at[2]),
        pltpu.make_async_copy(table_hbm, table, in_sem.at[3]),
    ]
    for copy in inputs:
        copy.start()
    for e in range(steps - 1):
        lnd[e][...] = jnp.zeros_like(lnd[e])

    def there(x, y):
        return {"tx": x, "ty": y}

    def peer(d):
        return lax.rem(me + d, n)

    barrier = pltpu.get_barrier_semaphore()
    for d in range(1, n):
        pl.semaphore_signal(barrier, inc=1, device_id={"freq": peer(d)}, device_id_type=MESH)
    for x in (up, tx, down):
        for y in (left, ty, right):
            if x is not tx or y is not ty:
                pl.semaphore_signal(barrier, inc=1, device_id=there(x, y), device_id_type=MESH)

    def remote(src, dst, send, recv, to):
        return pltpu.make_async_remote_copy(
            src_ref=src, dst_ref=dst, send_sem=send, recv_sem=recv, device_id=to, device_id_type=MESH
        )

    def wait_for(ref, sem):
        pltpu.make_async_copy(ref, ref, sem).wait()

    def chunk_at(ref, c):
        if per == 1:
            return ref.at[:, pl.ds(lax.div(c, col_tiles), 1), pl.ds(lax.rem(c, col_tiles), 1)]
        high = per // col_tiles
        return ref.at[:, pl.ds(c * high, high)]

    def scatter(g):
        for d in range(1, n):
            to = peer(d)
            remote(
                chunk_at(src[g], lax.rem(to, chunks)), land[g].at[d], rs_send.at[g], rs_recv.at[g], {"freq": to}
            ).start()

    def reduce_and_gather(g):
        wait_for(land[g].at[1:n], rs_recv.at[g])
        total = chunk_at(src[g], mine)[...]
        for d in range(1, n):
            total = total + land[g][d]
        here = chunk_at(dst[g], mine)
        here[...] = total
        for d in range(1, chunks):
            remote(here, here, ag_send.at[g], ag_recv.at[g], {"freq": group + lax.rem(mine + d, chunks)}).start()

    def gather_wait(g, sem):
        wait_for(land[g].at[1:chunks], sem.at[g])

    halo = [DEG + w for w in outs[:-1]]

    def rows_up(e):
        w = halo[e]
        return remote(wv[e].at[:, :, 0:w], lnd[e].at[:, :, 0:w], halo_send.at[e, 0], halo_recv.at[e, 0], there(up, ty))

    def rows_down(e):
        w = halo[e]
        return remote(
            wv[e].at[:, :, rows - w : rows],
            lnd[e].at[:, :, w : 2 * w],
            halo_send.at[e, 1],
            halo_recv.at[e, 1],
            there(down, ty),
        )

    def columns(e):
        w = halo[e]
        copies = []
        for i, pk, landing, y in ((2, pk_l[e], in_r[e], left), (3, pk_r[e], in_l[e], right)):
            for src, dst, x in (
                (pk, landing.at[0:rows], tx),
                (pk.at[0:w], landing.at[rows : rows + w], up),
                (pk.at[rows - w : rows], landing.at[rows + w : rows + 2 * w], down),
            ):
                copies.append(remote(src, dst, halo_send.at[e, i], halo_recv.at[e, i], there(x, y)))
        return copies

    def send_halos(e):
        packed_l = packed_r = None
        lane = lax.broadcasted_iota(jnp.int32, (rows, LANES), 1)
        for i in range(fields):
            c, f = i // freqs, i % freqs
            start = wv[e][c, f, :, 0:LANES]
            end = wv[e][c, f, :, cols - LANES : cols]
            if i == 0:
                packed_l, packed_r = start, end
            else:
                packed_l = jnp.where(lane // GROUP == i, pltpu.roll(start, i * GROUP, 1), packed_l)
                packed_r = jnp.where(lane // GROUP == i - 1, pltpu.roll(end, i * GROUP, 1), packed_r)
        pk_l[e][...] = packed_l
        pk_r[e][...] = packed_r
        return lambda: start_halos(e)

    def start_halos(e):
        pl.when(tx > 0)(lambda: rows_up(e).start())
        pl.when(tx < n_tx - 1)(lambda: rows_down(e).start())
        for copy in columns(e):
            copy.start()

    def halo_recv_wait(e):
        pl.when(tx < n_tx - 1)(lambda: rows_up(e).wait_recv())
        pl.when(tx > 0)(lambda: rows_down(e).wait_recv())
        wait_for(in_r[e], halo_recv.at[e, 2])
        wait_for(in_l[e], halo_recv.at[e, 3])

    def halo_send_wait(e):
        pl.when(tx > 0)(lambda: rows_up(e).wait_send())
        pl.when(tx < n_tx - 1)(lambda: rows_down(e).wait_send())
        wait_for(in_r[e], halo_send.at[e, 2])
        wait_for(in_l[e], halo_send.at[e, 3])

    late = steps - 2

    def side_copies(g):
        if g == 0:
            pieces = [
                (0, bins.at[late : late + 1, 0:side], bins_dn, up, ty),
                (1, bins.at[late : late + 1, rows - side : rows], bins_up, down, ty),
            ]
            for i, landing, cs, y in (
                (2, bins_r, slice(0, LANES), left),
                (3, bins_l, slice(cols - LANES, cols), right),
            ):
                pieces += [
                    (i, bins.at[late : late + 1, :, cs], landing.at[:, 0:rows], tx, y),
                    (i, bins.at[late : late + 1, 0:side, cs], landing.at[:, rows : rows + side], up, y),
                    (i, bins.at[late : late + 1, rows - side : rows, cs], landing.at[:, rows + side : rows + 2 * side], down, y),
                ]
        else:
            high = side_tiles
            cut = dst[1].at[late - 1 : late]
            pieces = [
                (0, cut.at[:, 0:high], frac_dn, up, ty),
                (1, cut.at[:, row_tiles - high : row_tiles], frac_up, down, ty),
            ]
            for i, landing, ct, y in ((2, frac_r, 0, left), (3, frac_l, col_tiles - 1, right)):
                pieces += [
                    (i, cut.at[:, :, ct], landing.at[:, 0:row_tiles], tx, y),
                    (i, cut.at[:, 0:high, ct], landing.at[:, row_tiles : row_tiles + high], up, y),
                    (
                        i,
                        cut.at[:, row_tiles - high : row_tiles, ct],
                        landing.at[:, row_tiles + high : row_tiles + 2 * high],
                        down,
                        y,
                    ),
                ]
        return [remote(a, b, side_send.at[g, i], side_recv.at[g, i], there(x, y)) for i, a, b, x, y in pieces]

    def side_wait(g, sem):
        for i, landing in enumerate(((bins_dn, bins_up, bins_r, bins_l), (frac_dn, frac_up, frac_r, frac_l))[g]):
            wait_for(landing, sem.at[g, i])

    def place(s, r):
        high = outs[s] // 8
        if r < row_tiles:
            return 0, r
        if r < row_tiles + high:
            return 1, r - row_tiles
        return 2, r - 2 * high

    def grid(s):
        high = outs[s] // 8
        return [
            (r, c) for r in range(row_tiles + 2 * high) for c in range(col_tiles + (1 if high else 0))
        ]

    lane8 = lax.broadcasted_iota(jnp.int32, (8, LANES), 1)

    def bins_tile(s, r, c):
        part, t = place(s, r)
        b = t - (row_tiles - side_tiles) if part == 2 else t
        if c < col_tiles:
            cs = slice(LANES * c, LANES * c + LANES)
            if part == 0:
                return bins[s, 8 * t : 8 * t + 8, cs]
            return (bins_dn, bins_up)[part - 1][s - late, 8 * b : 8 * b + 8, cs]
        at = (0, rows, rows + side)[part] + 8 * b
        return jnp.where(lane8 < LANES // 2, bins_r[s - late, at : at + 8], bins_l[s - late, at : at + 8])

    def frac_tile(s, r, c):
        part, t = place(s, r)
        b = t - (row_tiles - side_tiles) if part == 2 else t
        if c < col_tiles:
            if part == 0:
                return dst[0][0, t, c] if s == 0 else dst[1][s - 1, t, c]
            return (frac_dn, frac_up)[part - 1][s - late, b, c]
        at = (0, row_tiles, row_tiles + side_tiles)[part] + b
        return jnp.where(lane8 < LANES // 2, frac_r[s - late, at], frac_l[s - late, at])

    inputs[0].wait()
    per_slab = slabs.shape[0]
    for j in range(steps):
        owner = owners[j]
        chosen = src[0].at[0] if j == 0 else src[1].at[j - 1]
        for r in range(row_tiles):
            for c in range(col_tiles):
                value = jnp.zeros((8, LANES), jnp.float32)
                for i in range(per_slab):
                    tile = slabs[i, 8 * r : 8 * r + 8, LANES * c : LANES * c + LANES]
                    value = jnp.where(jnp.full((8, LANES), owner) == me * per_slab + i, tile, value)
                chosen[r, c] = value

    inputs[1].wait()
    send_halos(0)
    inputs[2].wait()
    pl.semaphore_wait(barrier, n - 1 + 8)
    scatter(0)
    start_halos(0)
    scatter(1)
    for copy in side_copies(0):
        copy.start()

    inputs[3].wait()
    tab_a[...] = jnp.zeros_like(tab_a)
    for c in range(2):
        for f in range(freqs):
            tab_a[c * freqs + f, 0:orders, 0 : table.shape[3]] = table[c, :, f]
    for i in range(fields):
        tab_d[i] = pltpu.roll(tab_a[i], LANES - 1, 1) - tab_a[i]

    ext_cols = cols + LANES
    c = lax.broadcasted_iota(jnp.int32, (8, ext_cols), 1)
    beside = jnp.where(c >= cols + LANES // 2, no_left, jnp.where(c >= cols, no_right, 0))
    for i, no_row in enumerate((0, no_down, no_up)):
        mask[i] = jnp.where(beside + no_row > 0, 0.0, 0.25)

    def quarter(w):
        high = w // 8
        return jnp.concatenate([mask[0]] * row_tiles + [mask[1]] * high + [mask[2]] * high, axis=0)

    def lookup(s):
        def one(i, carry):
            for r, c in grid(s):
                rs, cs = slice(8 * r, 8 * r + 8), slice(LANES * c, LANES * c + LANES)
                index = bins_tile(s, r, c)
                for k in range(orders):
                    for tab, co in ((tab_a, co_a[s]), (tab_d, co_d[s])):
                        row = jnp.broadcast_to(tab[i, k : k + 1, :], (8, LANES))
                        co[i, k, rs, cs] = jnp.take_along_axis(row, index, axis=1, mode="promise_in_bounds")
            return carry

        lax.fori_loop(0, fields, one, 0)

    def unpack(e):
        w = halo[e]
        ext = rows + 2 * w
        lane = lax.broadcasted_iota(jnp.int32, (ext, LANES), 1)
        one_roll = 2 * w <= GROUP
        if one_roll:
            both = jnp.where(lax.rem(lane, GROUP) < GROUP // 2, in_r[e][...], in_l[e][...])
        for i in range(fields):
            by = (LANES - i * GROUP) % LANES
            turn = (lambda v: pltpu.roll(v, by, 1)) if by else (lambda v: v)
            if one_roll:
                beyond = turn(both)
            else:
                beyond = jnp.where(lane < LANES // 2, turn(in_r[e][...]), turn(in_l[e][...]))
            own = jnp.concatenate([wv[e][i // freqs, i % freqs], lnd[e][i // freqs, i % freqs]], axis=0)
            t = jnp.concatenate([own, beyond], axis=1)
            first[e][i] = jnp.where(quarter(w) > 0.0, t, 0.0)

    def recurrence(s):
        w = outs[s] + DEG
        ext = rows + 2 * w

        def term(k, i):
            return first[s][i] if k == 0 else tk[k - 1, i, 0:ext]

        for k in range(1, orders):
            twice, summed, moved = [], [], []
            for i in range(fields):
                t = term(k - 1, i)
                twice.append(t + t)
                summed.append(twice[i] + (pltpu.roll(t, 1, 0) + pltpu.roll(t, ext - 1, 0)))
            for i in range(fields):
                moved.append(pltpu.roll(summed[i], 1, 1) + pltpu.roll(summed[i], ext_cols - 1, 1))
            for i in range(fields):
                smooth = (summed[i] + summed[i] + moved[i]) * quarter(w)
                if k == 1:
                    tk[0, i, 0:ext] = 0.5 * (smooth - twice[i])
                else:
                    tk[k - 1, i, 0:ext] = (smooth - term(k - 2, i)) - twice[i]

    def image_at(s):
        return (2, s) if s < late else (3 + s - late, 0)

    scale = 1.0 / math.sqrt(freqs * n)

    def combine(s):
        g, j = image_at(s)
        image = src[g].at[j]
        for r, c in grid(s):
            rs, cs = slice(8 * r, 8 * r + 8), slice(LANES * c, LANES * c + LANES)
            part, t = place(s, r)
            at = 8 * r if part < 2 else 8 * r + 2 * DEG
            ts = slice(at, at + 8)
            fraction = frac_tile(s, r, c)
            summed = None
            for f in range(freqs):
                re = im = None
                for k in range(orders):
                    t_re = first[s][f, ts, cs] if k == 0 else tk[k - 1, f, ts, cs]
                    t_im = first[s][freqs + f, ts, cs] if k == 0 else tk[k - 1, freqs + f, ts, cs]
                    c_re = co_a[s][f, k, rs, cs] + fraction * co_d[s][f, k, rs, cs]
                    c_im = co_a[s][freqs + f, k, rs, cs] + fraction * co_d[s][freqs + f, k, rs, cs]
                    add_re = c_re * t_re - c_im * t_im
                    add_im = c_re * t_im + c_im * t_re
                    re = add_re if k == 0 else re + add_re
                    im = add_im if k == 0 else im + add_im
                if s == steps - 1:
                    wave_out[0, f, rs, cs] = re
                    wave_out[1, f, rs, cs] = im
                elif s < late:
                    wv[s + 1][0, f, rs, cs] = re
                    wv[s + 1][1, f, rs, cs] = im
                else:
                    first[s + 1][f, rs, cs] = re
                    first[s + 1][freqs + f, rs, cs] = im
                summed = re if f == 0 else summed + re
            if part == 0 and c < col_tiles:
                image[t, c] = summed * scale

    lookup(0)
    reduce_and_gather(0)
    for s in range(steps):
        if s <= late:
            halo_recv_wait(s)
            unpack(s)
        recurrence(s)
        if s < 2:
            gather_wait(s, ag_recv)
        if s == late:
            side_wait(1, side_recv)
        combine(s)
        if s < late:
            send_halos(s + 1)
            start_halos(s + 1)
        if s == 0:
            reduce_and_gather(1)
            lookup(1)
            lookup(steps - 1)
        elif s == 1:
            for copy in side_copies(1):
                copy.start()
        if s == late - 1:
            scatter(2)
            side_wait(0, side_recv)
        if 1 <= s < late:
            lookup(s + 1)
        if s == late:
            scatter(3)
    scatter(4)
    for g in range(2, 5):
        reduce_and_gather(g)

    def put_image(s):
        g, j = image_at(s)
        for r in range(row_tiles):
            for c in range(col_tiles):
                images[s, 8 * r : 8 * r + 8, LANES * c : LANES * c + LANES] = dst[g][j, r, c]

    for g in range(2, 4):
        gather_wait(g, ag_recv)
    for s in range(steps - 1):
        put_image(s)
    for e in range(steps - 1):
        halo_send_wait(e)
    for g in range(2):
        side_wait(g, side_send)
    for g in range(5):
        wait_for(land[g].at[1:n], rs_send.at[g])
    for g in range(4):
        gather_wait(g, ag_send)
    gather_wait(4, ag_recv)
    put_image(steps - 1)
    gather_wait(4, ag_send)


def solution(mesh):
    n, n_tx, n_ty = (mesh.shape[axis] for axis in ("freq", "tx", "ty"))

    def on_device(wavefield, coef_table, velocity_bins, slab_fracs, owners):
        _, freqs, rows, cols = wavefield.shape
        orders = coef_table.shape[2]
        steps = velocity_bins.shape[0]
        row_tiles, col_tiles = rows // 8, cols // LANES
        tiles = row_tiles * col_tiles
        per = tiles // min(n, tiles)
        chunk = (per // col_tiles, col_tiles) if per > 1 else (1, 1)
        outs = widths(steps)
        side = max(outs)
        fields = 2 * freqs
        ext_cols = cols + LANES
        f32, i32 = jnp.float32, jnp.int32
        vmem = pl.BlockSpec(memory_space=pltpu.VMEM)
        hbm = pl.BlockSpec(memory_space=pltpu.HBM)
        dma = pltpu.SemaphoreType.DMA
        tile = (8, LANES)

        def ext(s):
            return rows + 2 * (outs[s] + DEG)

        coefs = [
            pltpu.VMEM((fields, orders, rows + 2 * w, cols + (LANES if w else 0)), f32) for w in outs
        ]
        scratch = [pltpu.VMEM((2, orders, freqs, coef_table.shape[3]), f32)]
        scratch += [pltpu.VMEM(velocity_bins.shape, i32), pltpu.VMEM(slab_fracs.shape, f32)]
        scratch += [pltpu.VMEM((2, freqs, rows, cols), f32) for e in range(steps - 1)]
        scratch += [pltpu.VMEM((2, freqs, ext(e) - rows, cols), f32) for e in range(steps - 1)]
        scratch += [pltpu.VMEM((rows, LANES), f32) for _ in range(2 * steps - 2)]
        scratch += [pltpu.VMEM((ext(e), LANES), f32) for e in [*range(steps - 1)] * 2]
        scratch += [pltpu.VMEM((fields, ext(s), ext_cols), f32) for s in range(steps)]
        scratch += coefs + coefs
        scratch += [
            pltpu.VMEM((orders - 1, fields, max(map(ext, range(steps))), ext_cols), f32),
            pltpu.VMEM((3, 8, ext_cols), f32),
            pltpu.VMEM((fields, 16, LANES), f32),
            pltpu.VMEM((fields, 16, LANES), f32),
        ]
        high = side // 8
        scratch += [pltpu.VMEM((1, side, cols), i32) for _ in range(2)]
        scratch += [pltpu.VMEM((1, rows + 2 * side, LANES), i32) for _ in range(2)]
        scratch += [pltpu.VMEM((1, high, col_tiles) + tile, f32) for _ in range(2)]
        scratch += [pltpu.VMEM((1, row_tiles + 2 * high) + tile, f32) for _ in range(2)]
        for lead in ((), (n,), ()):
            shape = (chunk if lead else (row_tiles, col_tiles)) + tile
            scratch += [pltpu.VMEM(lead + (m,) + shape, f32) for m in (1, steps - 1, steps - 2, 1, 1)]
        scratch += [dma((4,)), dma((steps - 1, 4)), dma((steps - 1, 4)), dma((2, 4)), dma((2, 4))]
        scratch += [dma((5,)) for _ in range(4)]
        in_hbm = functools.partial(pltpu.with_memory_space_constraint, memory_space=pltpu.HBM)
        return pl.pallas_call(
            functools.partial(kernel, (n, n_tx, n_ty), outs),
            out_shape=(
                jax.ShapeDtypeStruct(wavefield.shape, f32),
                jax.ShapeDtypeStruct((steps, rows, cols), f32),
            ),
            in_specs=[pl.BlockSpec(memory_space=pltpu.SMEM), hbm, hbm, hbm, hbm],
            out_specs=(vmem, vmem),
            scratch_shapes=scratch,
            compiler_params=pltpu.CompilerParams(
                collective_id=0, has_side_effects=True, vmem_limit_bytes=40 * 1024 * 1024
            ),
        )(
            owners,
            in_hbm(wavefield),
            in_hbm(jnp.transpose(coef_table, (0, 2, 1, 3))),
            in_hbm(velocity_bins),
            in_hbm(slab_fracs),
        )

    in_specs = (
        P(None, "freq", "tx", "ty"),
        P(None, "freq", None, None),
        P(None, "tx", "ty"),
        P("freq", "tx", "ty"),
        P(),
    )
    out_specs = (P(None, "freq", "tx", "ty"), P(None, "tx", "ty"))
    return jax.shard_map(on_device, mesh=mesh, in_specs=in_specs, out_specs=out_specs, check_vma=False)
```

```python
import functools
import math

import jax
import jax.numpy as jnp
from jax import lax
from jax.experimental import pallas as pl
from jax.experimental.pallas import tpu as pltpu
from jax.sharding import PartitionSpec as P

MESH = pl.DeviceIdType.MESH
LANES = 128
GROUP = 32
DEG = 8


def widths(steps):
    return [0] * (steps - 2) + [DEG, 0]


def kernel(sizes, outs, *refs):
    n, n_tx, n_ty = sizes
    refs = list(refs)

    def take(count):
        got = refs[:count]
        del refs[:count]
        return got

    owners, wave_hbm, table_hbm, bins_hbm, slabs_hbm, wave_out, images = take(7)
    table, bins, slabs = take(3)
    wv, lnd, pk_l, pk_r, in_r, in_l = (take(len(outs) - 1) for _ in range(6))
    first, co_a, co_d = (take(len(outs)) for _ in range(3))
    tk, mask, tab_a, tab_d = take(4)
    bins_dn, bins_up, bins_r, bins_l, frac_dn, frac_up, frac_r, frac_l = take(8)
    src, land, dst = take(5), take(5), take(5)
    in_sem, halo_send, halo_recv, side_send, side_recv, rs_send, rs_recv, ag_send, ag_recv = take(9)

    me, tx, ty = lax.axis_index("freq"), lax.axis_index("tx"), lax.axis_index("ty")
    _, freqs, rows, cols = wave_hbm.shape
    steps = bins.shape[0]
    orders = table.shape[1]
    row_tiles, col_tiles = rows // 8, cols // LANES
    tiles = row_tiles * col_tiles
    chunks = min(n, tiles)
    per = tiles // chunks
    fields = 2 * freqs
    mine, group = lax.rem(me, chunks), lax.div(me, chunks) * chunks
    side = max(outs)
    side_tiles = side // 8

    up, down = lax.rem(tx + n_tx - 1, n_tx), lax.rem(tx + 1, n_tx)
    left, right = lax.rem(ty + n_ty - 1, n_ty), lax.rem(ty + 1, n_ty)
    no_down = jnp.where(tx == n_tx - 1, 1, 0)
    no_up = jnp.where(tx == 0, 1, 0)
    no_right = jnp.where(ty == n_ty - 1, 1, 0)
    no_left = jnp.where(ty == 0, 1, 0)

    def there(x, y):
        return {"tx": x, "ty": y}

    def peer(d):
        return lax.rem(me + d, n)

    barrier = pltpu.get_barrier_semaphore()
    for d in range(1, n):
        pl.semaphore_signal(barrier, inc=1, device_id={"freq": peer(d)}, device_id_type=MESH)

    inputs = [
        pltpu.make_async_copy(slabs_hbm, slabs, in_sem.at[0]),
        pltpu.make_async_copy(wave_hbm, wv[0], in_sem.at[1]),
        pltpu.make_async_copy(bins_hbm, bins, in_sem.at[2]),
        pltpu.make_async_copy(table_hbm, table, in_sem.at[3]),
    ]
    for copy in inputs:
        copy.start()
    for e in range(steps - 1):
        lnd[e][...] = jnp.zeros_like(lnd[e])
    for x in (up, tx, down):
        for y in (left, ty, right):
            if x is not tx or y is not ty:
                pl.semaphore_signal(barrier, inc=1, device_id=there(x, y), device_id_type=MESH)

    def remote(src, dst, send, recv, to):
        return pltpu.make_async_remote_copy(
            src_ref=src, dst_ref=dst, send_sem=send, recv_sem=recv, device_id=to, device_id_type=MESH
        )

    def wait_for(ref, sem):
        pltpu.make_async_copy(ref, ref, sem).wait()

    def chunk_at(ref, c):
        if per == 1:
            return ref.at[:, pl.ds(lax.div(c, col_tiles), 1), pl.ds(lax.rem(c, col_tiles), 1)]
        high = per // col_tiles
        return ref.at[:, pl.ds(c * high, high)]

    def scatter(g):
        for d in range(1, n):
            to = peer(d)
            remote(
                chunk_at(src[g], lax.rem(to, chunks)), land[g].at[d], rs_send.at[g], rs_recv.at[g], {"freq": to}
            ).start()

    def reduce_and_gather(g):
        wait_for(land[g].at[1:n], rs_recv.at[g])
        total = chunk_at(src[g], mine)[...]
        for d in range(1, n):
            total = total + land[g][d]
        here = chunk_at(dst[g], mine)
        here[...] = total
        for d in range(1, chunks):
            remote(here, here, ag_send.at[g], ag_recv.at[g], {"freq": group + lax.rem(mine + d, chunks)}).start()

    def gather_wait(g, sem):
        wait_for(land[g].at[1:chunks], sem.at[g])

    halo = [DEG + w for w in outs[:-1]]

    def rows_up(e):
        w = halo[e]
        return remote(wv[e].at[:, :, 0:w], lnd[e].at[:, :, 0:w], halo_send.at[e, 0], halo_recv.at[e, 0], there(up, ty))

    def rows_down(e):
        w = halo[e]
        return remote(
            wv[e].at[:, :, rows - w : rows],
            lnd[e].at[:, :, w : 2 * w],
            halo_send.at[e, 1],
            halo_recv.at[e, 1],
            there(down, ty),
        )

    def columns(e):
        w = halo[e]
        copies = []
        for i, pk, landing, y in ((2, pk_l[e], in_r[e], left), (3, pk_r[e], in_l[e], right)):
            for src, dst, x in (
                (pk, landing.at[0:rows], tx),
                (pk.at[0:w], landing.at[rows : rows + w], up),
                (pk.at[rows - w : rows], landing.at[rows + w : rows + 2 * w], down),
            ):
                copies.append(remote(src, dst, halo_send.at[e, i], halo_recv.at[e, i], there(x, y)))
        return copies

    def send_halos(e):
        packed_l = packed_r = None
        lane = lax.broadcasted_iota(jnp.int32, (rows, LANES), 1)
        for i in range(fields):
            c, f = i // freqs, i % freqs
            start = wv[e][c, f, :, 0:LANES]
            end = wv[e][c, f, :, cols - LANES : cols]
            if i == 0:
                packed_l, packed_r = start, end
            else:
                packed_l = jnp.where(lane // GROUP == i, pltpu.roll(start, i * GROUP, 1), packed_l)
                packed_r = jnp.where(lane // GROUP == i - 1, pltpu.roll(end, i * GROUP, 1), packed_r)
        pk_l[e][...] = packed_l
        pk_r[e][...] = packed_r
        return lambda: start_halos(e)

    def start_halos(e):
        pl.when(tx > 0)(lambda: rows_up(e).start())
        pl.when(tx < n_tx - 1)(lambda: rows_down(e).start())
        for copy in columns(e):
            copy.start()

    def halo_recv_wait(e):
        pl.when(tx < n_tx - 1)(lambda: rows_up(e).wait_recv())
        pl.when(tx > 0)(lambda: rows_down(e).wait_recv())
        wait_for(in_r[e], halo_recv.at[e, 2])
        wait_for(in_l[e], halo_recv.at[e, 3])

    def halo_send_wait(e):
        pl.when(tx > 0)(lambda: rows_up(e).wait_send())
        pl.when(tx < n_tx - 1)(lambda: rows_down(e).wait_send())
        wait_for(in_r[e], halo_send.at[e, 2])
        wait_for(in_l[e], halo_send.at[e, 3])

    late = steps - 2

    def side_copies(g):
        if g == 0:
            pieces = [
                (0, bins.at[late : late + 1, 0:side], bins_dn, up, ty),
                (1, bins.at[late : late + 1, rows - side : rows], bins_up, down, ty),
            ]
            for i, landing, cs, y in (
                (2, bins_r, slice(0, LANES), left),
                (3, bins_l, slice(cols - LANES, cols), right),
            ):
                pieces += [
                    (i, bins.at[late : late + 1, :, cs], landing.at[:, 0:rows], tx, y),
                    (i, bins.at[late : late + 1, 0:side, cs], landing.at[:, rows : rows + side], up, y),
                    (i, bins.at[late : late + 1, rows - side : rows, cs], landing.at[:, rows + side : rows + 2 * side], down, y),
                ]
        else:
            high = side_tiles
            cut = dst[1].at[late - 1 : late]
            pieces = [
                (0, cut.at[:, 0:high], frac_dn, up, ty),
                (1, cut.at[:, row_tiles - high : row_tiles], frac_up, down, ty),
            ]
            for i, landing, ct, y in ((2, frac_r, 0, left), (3, frac_l, col_tiles - 1, right)):
                pieces += [
                    (i, cut.at[:, :, ct], landing.at[:, 0:row_tiles], tx, y),
                    (i, cut.at[:, 0:high, ct], landing.at[:, row_tiles : row_tiles + high], up, y),
                    (
                        i,
                        cut.at[:, row_tiles - high : row_tiles, ct],
                        landing.at[:, row_tiles + high : row_tiles + 2 * high],
                        down,
                        y,
                    ),
                ]
        return [remote(a, b, side_send.at[g, i], side_recv.at[g, i], there(x, y)) for i, a, b, x, y in pieces]

    def side_wait(g, sem):
        for i, landing in enumerate(((bins_dn, bins_up, bins_r, bins_l), (frac_dn, frac_up, frac_r, frac_l))[g]):
            wait_for(landing, sem.at[g, i])

    def place(s, r):
        high = outs[s] // 8
        if r < row_tiles:
            return 0, r
        if r < row_tiles + high:
            return 1, r - row_tiles
        return 2, r - 2 * high

    def grid(s):
        high = outs[s] // 8
        return [
            (r, c) for r in range(row_tiles + 2 * high) for c in range(col_tiles + (1 if high else 0))
        ]

    lane8 = lax.broadcasted_iota(jnp.int32, (8, LANES), 1)

    def bins_tile(s, r, c):
        part, t = place(s, r)
        b = t - (row_tiles - side_tiles) if part == 2 else t
        if c < col_tiles:
            cs = slice(LANES * c, LANES * c + LANES)
            if part == 0:
                return bins[s, 8 * t : 8 * t + 8, cs]
            return (bins_dn, bins_up)[part - 1][s - late, 8 * b : 8 * b + 8, cs]
        at = (0, rows, rows + side)[part] + 8 * b
        return jnp.where(lane8 < LANES // 2, bins_r[s - late, at : at + 8], bins_l[s - late, at : at + 8])

    def frac_tile(s, r, c):
        part, t = place(s, r)
        b = t - (row_tiles - side_tiles) if part == 2 else t
        if c < col_tiles:
            if part == 0:
                return dst[0][0, t, c] if s == 0 else dst[1][s - 1, t, c]
            return (frac_dn, frac_up)[part - 1][s - late, b, c]
        at = (0, row_tiles, row_tiles + side_tiles)[part] + b
        return jnp.where(lane8 < LANES // 2, frac_r[s - late, at], frac_l[s - late, at])

    inputs[0].wait()
    per_slab = slabs.shape[0]
    for j in range(steps):
        owner = owners[j]
        chosen = src[0].at[0] if j == 0 else src[1].at[j - 1]
        for r in range(row_tiles):
            for c in range(col_tiles):
                value = jnp.zeros((8, LANES), jnp.float32)
                for i in range(per_slab):
                    tile = slabs[i, 8 * r : 8 * r + 8, LANES * c : LANES * c + LANES]
                    value = jnp.where(jnp.full((8, LANES), owner) == me * per_slab + i, tile, value)
                chosen[r, c] = value

    inputs[1].wait()
    send_halos(0)
    inputs[2].wait()
    pl.semaphore_wait(barrier, n - 1 + 8)
    scatter(0)
    start_halos(0)
    scatter(1)
    for copy in side_copies(0):
        copy.start()

    inputs[3].wait()
    tab_a[...] = jnp.zeros_like(tab_a)
    for c in range(2):
        for f in range(freqs):
            tab_a[c * freqs + f, 0:orders, 0 : table.shape[3]] = table[c, :, f]
    for i in range(fields):
        tab_d[i] = pltpu.roll(tab_a[i], LANES - 1, 1) - tab_a[i]

    ext_cols = cols + LANES
    c = lax.broadcasted_iota(jnp.int32, (8, ext_cols), 1)
    beside = jnp.where(c >= cols + LANES // 2, no_left, jnp.where(c >= cols, no_right, 0))
    for i, no_row in enumerate((0, no_down, no_up)):
        mask[i] = jnp.where(beside + no_row > 0, 0.0, 0.25)

    def quarter(w):
        high = w // 8
        return jnp.concatenate([mask[0]] * row_tiles + [mask[1]] * high + [mask[2]] * high, axis=0)

    def lookup(s):
        def one(i, carry):
            for r, c in grid(s):
                rs, cs = slice(8 * r, 8 * r + 8), slice(LANES * c, LANES * c + LANES)
                index = bins_tile(s, r, c)
                for k in range(orders):
                    for tab, co in ((tab_a, co_a[s]), (tab_d, co_d[s])):
                        row = jnp.broadcast_to(tab[i, k : k + 1, :], (8, LANES))
                        co[i, k, rs, cs] = jnp.take_along_axis(row, index, axis=1, mode="promise_in_bounds")
            return carry

        lax.fori_loop(0, fields, one, 0)

    def unpack(e):
        w = halo[e]
        ext = rows + 2 * w
        lane = lax.broadcasted_iota(jnp.int32, (ext, LANES), 1)
        one_roll = 2 * w <= GROUP
        if one_roll:
            both = jnp.where(lax.rem(lane, GROUP) < GROUP // 2, in_r[e][...], in_l[e][...])
        for i in range(fields):
            by = (LANES - i * GROUP) % LANES
            turn = (lambda v: pltpu.roll(v, by, 1)) if by else (lambda v: v)
            if one_roll:
                beyond = turn(both)
            else:
                beyond = jnp.where(lane < LANES // 2, turn(in_r[e][...]), turn(in_l[e][...]))
            own = jnp.concatenate([wv[e][i // freqs, i % freqs], lnd[e][i // freqs, i % freqs]], axis=0)
            t = jnp.concatenate([own, beyond], axis=1)
            first[e][i] = jnp.where(quarter(w) > 0.0, t, 0.0)

    def recurrence(s):
        w = outs[s] + DEG
        ext = rows + 2 * w

        def term(k, i):
            return first[s][i] if k == 0 else tk[k - 1, i, 0:ext]

        for k in range(1, orders):
            twice, summed, moved = [], [], []
            for i in range(fields):
                t = term(k - 1, i)
                twice.append(t + t)
                summed.append(twice[i] + (pltpu.roll(t, 1, 0) + pltpu.roll(t, ext - 1, 0)))
            for i in range(fields):
                moved.append(pltpu.roll(summed[i], 1, 1) + pltpu.roll(summed[i], ext_cols - 1, 1))
            for i in range(fields):
                smooth = (summed[i] + summed[i] + moved[i]) * quarter(w)
                if k == 1:
                    tk[0, i, 0:ext] = 0.5 * (smooth - twice[i])
                else:
                    t = (smooth - term(k - 2, i)) - twice[i]
                    below = rows + outs[s]
                    if k < orders - 1:
                        tk[k - 1, i, 0:ext] = t
                    else:
                        tk[k - 1, i, 0:below] = t[0:below]
                        if outs[s]:
                            tk[k - 1, i, ext - outs[s] : ext] = t[ext - outs[s] : ext]

    def image_at(s):
        return (2, s) if s < late else (3 + s - late, 0)

    scale = 1.0 / math.sqrt(freqs * n)

    def combine(s):
        g, j = image_at(s)
        image = src[g].at[j]
        for r, c in grid(s):
            rs, cs = slice(8 * r, 8 * r + 8), slice(LANES * c, LANES * c + LANES)
            part, t = place(s, r)
            at = 8 * r if part < 2 else 8 * r + 2 * DEG
            ts = slice(at, at + 8)
            fraction = frac_tile(s, r, c)
            summed = None
            for f in range(freqs):
                re = im = None
                for k in range(orders):
                    t_re = first[s][f, ts, cs] if k == 0 else tk[k - 1, f, ts, cs]
                    t_im = first[s][freqs + f, ts, cs] if k == 0 else tk[k - 1, freqs + f, ts, cs]
                    c_re = co_a[s][f, k, rs, cs] + fraction * co_d[s][f, k, rs, cs]
                    c_im = co_a[s][freqs + f, k, rs, cs] + fraction * co_d[s][freqs + f, k, rs, cs]
                    add_re = c_re * t_re - c_im * t_im
                    add_im = c_re * t_im + c_im * t_re
                    re = add_re if k == 0 else re + add_re
                    im = add_im if k == 0 else im + add_im
                if s == steps - 1:
                    wave_out[0, f, rs, cs] = re
                    wave_out[1, f, rs, cs] = im
                elif s < late:
                    wv[s + 1][0, f, rs, cs] = re
                    wv[s + 1][1, f, rs, cs] = im
                else:
                    first[s + 1][f, rs, cs] = re
                    first[s + 1][freqs + f, rs, cs] = im
                summed = re if f == 0 else summed + re
            if part == 0 and c < col_tiles:
                image[t, c] = summed * scale

    lookup(0)
    reduce_and_gather(0)
    for s in range(steps):
        if s <= late:
            halo_recv_wait(s)
            unpack(s)
        recurrence(s)
        if s < 2:
            gather_wait(s, ag_recv)
        if s == late:
            side_wait(1, side_recv)
        combine(s)
        if s < late:
            send_halos(s + 1)
            start_halos(s + 1)
        if s == 0:
            reduce_and_gather(1)
            lookup(1)
            lookup(steps - 1)
        elif s == 1:
            for copy in side_copies(1):
                copy.start()
        if s == late - 1:
            scatter(2)
            side_wait(0, side_recv)
        if 1 <= s < late:
            lookup(s + 1)
        if s == late:
            scatter(3)
    scatter(4)
    for g in range(2, 5):
        reduce_and_gather(g)

    def put_image(s):
        g, j = image_at(s)
        for r in range(row_tiles):
            for c in range(col_tiles):
                images[s, 8 * r : 8 * r + 8, LANES * c : LANES * c + LANES] = dst[g][j, r, c]

    for g in range(2, 4):
        gather_wait(g, ag_recv)
    for s in range(steps - 1):
        put_image(s)
    for e in range(steps - 1):
        halo_send_wait(e)
    for g in range(2):
        side_wait(g, side_send)
    for g in range(5):
        wait_for(land[g].at[1:n], rs_send.at[g])
    for g in range(4):
        gather_wait(g, ag_send)
    gather_wait(4, ag_recv)
    put_image(steps - 1)
    gather_wait(4, ag_send)


def solution(mesh):
    n, n_tx, n_ty = (mesh.shape[axis] for axis in ("freq", "tx", "ty"))

    def on_device(wavefield, coef_table, velocity_bins, slab_fracs, owners):
        _, freqs, rows, cols = wavefield.shape
        orders = coef_table.shape[2]
        steps = velocity_bins.shape[0]
        row_tiles, col_tiles = rows // 8, cols // LANES
        tiles = row_tiles * col_tiles
        per = tiles // min(n, tiles)
        chunk = (per // col_tiles, col_tiles) if per > 1 else (1, 1)
        outs = widths(steps)
        side = max(outs)
        fields = 2 * freqs
        ext_cols = cols + LANES
        f32, i32 = jnp.float32, jnp.int32
        vmem = pl.BlockSpec(memory_space=pltpu.VMEM)
        hbm = pl.BlockSpec(memory_space=pltpu.HBM)
        dma = pltpu.SemaphoreType.DMA
        tile = (8, LANES)

        def ext(s):
            return rows + 2 * (outs[s] + DEG)

        coefs = [
            pltpu.VMEM((fields, orders, rows + 2 * w, cols + (LANES if w else 0)), f32) for w in outs
        ]
        scratch = [pltpu.VMEM((2, orders, freqs, coef_table.shape[3]), f32)]
        scratch += [pltpu.VMEM(velocity_bins.shape, i32), pltpu.VMEM(slab_fracs.shape, f32)]
        scratch += [pltpu.VMEM((2, freqs, rows, cols), f32) for e in range(steps - 1)]
        scratch += [pltpu.VMEM((2, freqs, ext(e) - rows, cols), f32) for e in range(steps - 1)]
        scratch += [pltpu.VMEM((rows, LANES), f32) for _ in range(2 * steps - 2)]
        scratch += [pltpu.VMEM((ext(e), LANES), f32) for e in [*range(steps - 1)] * 2]
        scratch += [pltpu.VMEM((fields, ext(s), ext_cols), f32) for s in range(steps)]
        scratch += coefs + coefs
        scratch += [
            pltpu.VMEM((orders - 1, fields, max(map(ext, range(steps))), ext_cols), f32),
            pltpu.VMEM((3, 8, ext_cols), f32),
            pltpu.VMEM((fields, 16, LANES), f32),
            pltpu.VMEM((fields, 16, LANES), f32),
        ]
        high = side // 8
        scratch += [pltpu.VMEM((1, side, cols), i32) for _ in range(2)]
        scratch += [pltpu.VMEM((1, rows + 2 * side, LANES), i32) for _ in range(2)]
        scratch += [pltpu.VMEM((1, high, col_tiles) + tile, f32) for _ in range(2)]
        scratch += [pltpu.VMEM((1, row_tiles + 2 * high) + tile, f32) for _ in range(2)]
        for lead in ((), (n,), ()):
            shape = (chunk if lead else (row_tiles, col_tiles)) + tile
            scratch += [pltpu.VMEM(lead + (m,) + shape, f32) for m in (1, steps - 1, steps - 2, 1, 1)]
        scratch += [dma((4,)), dma((steps - 1, 4)), dma((steps - 1, 4)), dma((2, 4)), dma((2, 4))]
        scratch += [dma((5,)) for _ in range(4)]
        in_hbm = functools.partial(pltpu.with_memory_space_constraint, memory_space=pltpu.HBM)
        return pl.pallas_call(
            functools.partial(kernel, (n, n_tx, n_ty), outs),
            out_shape=(
                jax.ShapeDtypeStruct(wavefield.shape, f32),
                jax.ShapeDtypeStruct((steps, rows, cols), f32),
            ),
            in_specs=[pl.BlockSpec(memory_space=pltpu.SMEM), hbm, hbm, hbm, hbm],
            out_specs=(vmem, vmem),
            scratch_shapes=scratch,
            compiler_params=pltpu.CompilerParams(
                collective_id=0, has_side_effects=True, vmem_limit_bytes=40 * 1024 * 1024
            ),
        )(
            in_hbm(owners),
            in_hbm(wavefield),
            in_hbm(jnp.transpose(coef_table, (0, 2, 1, 3))),
            in_hbm(velocity_bins),
            in_hbm(slab_fracs),
        )

    in_specs = (
        P(None, "freq", "tx", "ty"),
        P(None, "freq", None, None),
        P(None, "tx", "ty"),
        P("freq", "tx", "ty"),
        P(),
    )
    out_specs = (P(None, "freq", "tx", "ty"), P(None, "tx", "ty"))
    return jax.shard_map(on_device, mesh=mesh, in_specs=in_specs, out_specs=out_specs, check_vma=False)
```
